512 devices in a mesh: sess: 32 (over y, x), tensor: 16 (over z, core).
Axes of the slice: x: 4, y: 8, z: 8, core: 2. Of those that a mesh axis runs over, the one named last changes fastest.
Arguments:
- hidden: bfloat16 [32, 8192], P('sess'), may hold values from -6 to 6
- key_value_weight: bfloat16 [8192, 2048], P(None, 'tensor'), may hold values from -0.0625 to 0.0625
- adapter_down_maps: bfloat16 [64, 2, 64, 8192], P('sess', None, 'tensor'), may hold values from -0.0625 to 0.0625
- adapter_up_maps: bfloat16 [64, 2, 64, 1024], P('sess', None, 'tensor'), may hold values from -0.75 to 0.75
- session_slot: int32 [32], replicated, may hold values from 0 to 63, as said below
- lengths: int32 [32], P('sess'), may hold values from 2048 to 4095, as said below
- queries: bfloat16 [32, 8192], P('sess', 'tensor'), may hold values from -400 to 400
- cached_key_rows: bfloat16 [32, 4096, 1024], P('sess', 'tensor'), may hold values from -12 to 12
- cached_value_rows: bfloat16 [32, 4096, 1024], P('sess', 'tensor'), may hold values from -6 to 6
Outputs:
- new_key_value: bfloat16 [32, 2048], P('sess', 'tensor')
- attended: bfloat16 [32, 8192], P('sess', 'tensor')
The draws below stay inside these ranges and needn't reach their ends.
Inputs may be any that keep to these rules, and one draw needn't show every extreme that they name: `session_slot`: the sessions' slots are distinct; slot q lives on index q // 2 of sess; in every draw some index of sess holds the adapters of 2 sessions. The new token takes position lengths[s]; some session has 4095.
All inputs are finite; a program needn't handle non-finite values.
Results may differ from the reference program's by a relative error of at most 0.014.
Values may be sent and summed in bfloat16 or wider, within the bound.
No kernel may reach another device: no remote copies, remote signals or barrier semaphores. Data moves between devices by JAX's collectives and lax.ppermute only.
A program may use at most 64 MiB of HBM per device.

```python
import math
import jax
import jax.numpy as jnp
from jax import lax

MODEL_WIDTH = 8192
QH = 64
KVH = 8
HD = 128
ADAPTER_RANK = 64
CTX = 4096
ADAPTER_SLOTS = 2
KEY_VALUE_WIDTH = 1024
SESSIONS = 32
TOTAL_SLOTS = 64


def raw_row(base_key, session, position):
    folded = jax.random.fold_in(jax.random.fold_in(base_key, session), position)
    return jnp.clip(jax.random.normal(folded, (KVH * HD,), jnp.float32), -4.0, 4.0)


def session_scales(key, low_end, high_end):
    sampled = jnp.exp(jax.random.uniform(jax.random.fold_in(key, 14), (SESSIONS,), jnp.float32, math.log(low_end), math.log(high_end)))
    top_one = jax.random.randint(jax.random.fold_in(key, 15), (), 0, SESSIONS)
    step_by = jax.random.randint(jax.random.fold_in(key, 16), (), 1, SESSIONS)
    low_one = (top_one + step_by) % SESSIONS
    places = jnp.arange(SESSIONS, dtype=jnp.int32)
    sampled = jnp.where(places == top_one, high_end, sampled)
    sampled = jnp.where(places == low_one, low_end, sampled)
    return sampled


def draw_cached_key_rows(key, part):
    base_key = jax.random.fold_in(key, 11)
    sessions_all = jnp.arange(SESSIONS, dtype=jnp.int32)
    positions_all = jnp.arange(CTX, dtype=jnp.int32)
    rows = jax.vmap(lambda session: jax.vmap(lambda position: raw_row(base_key, session, position))(positions_all))(sessions_all)
    rows = rows * session_scales(key, 1.0, 3.0)[:, None, None]
    return jnp.clip(rows, -12.0, 12.0).astype(jnp.bfloat16)


def draw_queries(key, part):
    entries = jnp.clip(jax.random.normal(jax.random.fold_in(key, 21), (SESSIONS, QH * HD), jnp.float32), -4.0, 4.0)
    entries = entries * 32.0
    return entries.astype(jnp.bfloat16)


def draw_session_slot(key, part):
    owners = TOTAL_SLOTS // ADAPTER_SLOTS
    owner_ids = jnp.arange(owners, dtype=jnp.int32)
    owner_weight = jax.random.randint(jax.random.fold_in(key, 31), (owners,), 0, 4)
    favored = jax.random.randint(jax.random.fold_in(key, 32), (), 0, owners)
    owner_weight = jnp.where(owner_ids == owners - 1, 4, owner_weight)
    owner_weight = jnp.where(owner_ids == favored, 8, owner_weight)
    owner_weight = jnp.where(owner_ids == owners // 2, 8, owner_weight)
    noise = jax.random.randint(jax.random.fold_in(key, 33), (TOTAL_SLOTS,), 0, 1024)
    slot_ids = jnp.arange(TOTAL_SLOTS, dtype=jnp.int32)
    scores = (owner_weight[slot_ids // ADAPTER_SLOTS] * 1024 + noise) * TOTAL_SLOTS + slot_ids
    chosen = lax.top_k(scores, SESSIONS)[1]
    order = jax.random.permutation(jax.random.fold_in(key, 34), SESSIONS)
    result = chosen[order].astype(jnp.int32)
    far_owned = (result // ADAPTER_SLOTS == owners // 2).astype(jnp.int32)
    spot = jnp.argmax(far_owned).astype(jnp.int32)
    first_value = result[0]
    spot_value = result[spot]
    places = jnp.arange(SESSIONS, dtype=jnp.int32)
    result = jnp.where(places == spot, first_value, result)
    result = jnp.where(places == 0, spot_value, result)
    return result.astype(jnp.int32)


def draw_lengths(key, part):
    drawn = jax.random.randint(jax.random.fold_in(key, 41), (SESSIONS,), CTX // 2, CTX)
    longest = jax.random.randint(jax.random.fold_in(key, 42), (), 0, SESSIONS)
    return jnp.where(jnp.arange(SESSIONS, dtype=jnp.int32) == longest, CTX - 1, drawn).astype(jnp.int32)


def levels(key, dims, cuts, low, largest):
    factor_of, own = 1.0, jax.random.fold_in(key, 6)
    for axis_at, shards_of in cuts:
        steps = jnp.exp(jax.random.uniform(jax.random.fold_in(own, axis_at), (shards_of,), jnp.float32, low / len(cuts), largest / len(cuts)))
        factor_of = factor_of * jnp.repeat(steps, dims[axis_at] // shards_of).reshape([-1 if axis == axis_at else 1 for axis in range(len(dims))])
    return factor_of


def gaussian(stream_key, extent, scale, reach, pieces=(), kind=jnp.bfloat16):
    gain = levels(stream_key, extent, pieces, -0.22, 0.18) if pieces else 1.0
    entries = jax.random.normal(stream_key, extent, jnp.float32) * scale * gain
    return jnp.minimum(jnp.maximum(entries, -reach), reach).astype(kind)


def setup_inputs(seed: int = 0) -> dict:
    key_of = jax.random.split(jax.random.key(seed), 10)
    hidden = gaussian(key_of[0], (SESSIONS, MODEL_WIDTH), 1.0, 6.0, ((0, 32),))
    key_value_weight = gaussian(key_of[1], (MODEL_WIDTH, 2 * KEY_VALUE_WIDTH), MODEL_WIDTH ** -0.5, 0.0625, ((1, 16),))
    adapter_down_maps = gaussian(key_of[2], (TOTAL_SLOTS, 2, ADAPTER_RANK, MODEL_WIDTH), MODEL_WIDTH ** -0.5, 0.0625, ((0, 32), (2, 16)))
    adapter_up_maps = gaussian(key_of[3], (TOTAL_SLOTS, 2, ADAPTER_RANK, KEY_VALUE_WIDTH), ADAPTER_RANK ** -0.5, 0.75, ((0, 32), (2, 16)))
    session_slot = draw_session_slot(jax.random.fold_in(key_of[9], 71), 0)
    lengths = draw_lengths(jax.random.fold_in(key_of[9], 71), 0)
    queries = draw_queries(jax.random.fold_in(key_of[9], 71), 0)
    cached_key_rows = draw_cached_key_rows(jax.random.fold_in(key_of[9], 71), 0)
    cached_value_rows = gaussian(key_of[8], (SESSIONS, CTX, KEY_VALUE_WIDTH), 1.0, 6.0, ((0, 32), (1, 16)))
    return dict(hidden=hidden, key_value_weight=key_value_weight, adapter_down_maps=adapter_down_maps, adapter_up_maps=adapter_up_maps, session_slot=session_slot, lengths=lengths, queries=queries, cached_key_rows=cached_key_rows, cached_value_rows=cached_value_rows)


ADAPTER_SCALE = 0.5
ROPE_BASE = 500000.0
MASKED = -1e+30

def apply_rotation(columns_in, lengths, first_column):
    row_count = columns_in.shape[0]
    column_count = columns_in.shape[1]
    head_count = column_count // HD
    half_width = HD // 2
    shaped = columns_in.reshape(row_count, head_count, 2, half_width)
    indices = jnp.arange(half_width, dtype=jnp.float32)
    inverse = jnp.exp(-(2.0 * indices / HD) * math.log(ROPE_BASE))
    angles = lengths.astype(jnp.float32)[:, None] * inverse[None, :]
    cosine = jnp.cos(angles)[:, None, :]
    sine_part = jnp.sin(angles)[:, None, :]
    former = shaped[:, :, 0, :]
    latter = shaped[:, :, 1, :]
    turned = jnp.stack([former * cosine - latter * sine_part, latter * cosine + former * sine_part], axis=2)
    head_ids = first_column // HD + jnp.arange(head_count, dtype=jnp.int32)
    is_keyed = (head_ids < KVH)[None, :, None, None]
    return jnp.where(is_keyed, turned, shaped).reshape(row_count, column_count)

def reference(hidden, key_value_weight, adapter_down_maps, adapter_up_maps, session_slot, lengths, queries, cached_key_rows, cached_value_rows):
    kv_width = KVH * HD
    group = QH // KVH
    base_output = jnp.dot(hidden, key_value_weight, preferred_element_type=jnp.float32)

    def adapt(paired):
        hidden_row, slot_number = paired
        down_matrix = adapter_down_maps[slot_number].astype(jnp.float32)
        lowrank_input = jnp.einsum('d,krd->kr', hidden_row.astype(jnp.float32), down_matrix, precision=lax.Precision.HIGHEST)
        lowrank_input = lax.optimization_barrier(lowrank_input.astype(jnp.bfloat16)).astype(jnp.float32)
        up_matrix = adapter_up_maps[slot_number].astype(jnp.float32)
        lifted = jnp.einsum('kr,krc->kc', lowrank_input, up_matrix, precision=lax.Precision.HIGHEST)
        return lifted.reshape(2 * kv_width)
    adapter_delta = lax.map(adapt, (hidden, session_slot))
    new_key_value = apply_rotation(base_output + ADAPTER_SCALE * adapter_delta, lengths, 0).astype(jnp.bfloat16)

    def attend(bundle):
        query_row, keys_row, values_row, length, fresh = bundle
        positions = jnp.arange(CTX, dtype=jnp.int32)
        landing = (positions == length)[:, None]
        keys_row = jnp.where(landing, fresh[None, :kv_width], keys_row)
        values_row = jnp.where(landing, fresh[None, kv_width:], values_row)
        query_heads = query_row.astype(jnp.float32).reshape(KVH, group, HD)
        key_heads = keys_row.astype(jnp.float32).reshape(CTX, KVH, HD)
        scores = jnp.einsum('gjd,pgd->gjp', query_heads, key_heads, precision=lax.Precision.HIGHEST) * (1.0 / math.sqrt(HD))
        live = (positions <= length)[None, None, :]
        scores = jnp.where(live, scores, MASKED)
        highest = lax.optimization_barrier(jnp.max(scores, axis=2, keepdims=True))
        weights = jnp.where(live, jnp.exp(scores - highest), 0.0)
        denom = lax.optimization_barrier(jnp.sum(weights, axis=2))
        rounded = lax.optimization_barrier(weights.astype(jnp.bfloat16)).astype(jnp.float32)
        value_heads = values_row.astype(jnp.float32).reshape(CTX, KVH, HD)
        summed = jnp.einsum('gjp,pgd->gjd', rounded, value_heads, precision=lax.Precision.HIGHEST)
        return (summed / denom[:, :, None]).reshape(QH * HD).astype(jnp.bfloat16)
    attended = lax.map(attend, (queries, cached_key_rows, cached_value_rows, lengths, new_key_value))
    return (new_key_value, attended)
```

```python
import math

import jax
import jax.numpy as jnp
from jax import lax
from jax.sharding import PartitionSpec as P

QH = 64
KVH = 8
HD = 128
ADAPTER_SCALE = 0.5
ROPE_BASE = 500000.0
MASKED = -1e30


def rotate_head(row, cosine, sine):
    half = HD // 2
    a = row[:half]
    b = row[half:]
    return jnp.concatenate([a * cosine - b * sine, b * cosine + a * sine])


def local(
    hidden,
    key_value_weight,
    adapter_down_maps,
    adapter_up_maps,
    session_slot,
    lengths,
    queries,
    cached_key_rows,
    cached_value_rows,
):
    f32 = jnp.float32
    bf16 = jnp.bfloat16
    n_sess = lax.axis_size("sess")
    n_tensor = lax.axis_size("tensor")
    o = lax.axis_index("sess")
    t = lax.axis_index("tensor")
    slots, two, ranks, width = adapter_down_maps.shape
    kv_width = KVH * HD
    group = QH // KVH
    own_heads = QH // n_tensor
    span = cached_key_rows.shape[1]
    length = lengths[0]

    hidden_all = lax.all_to_all(
        jnp.broadcast_to(hidden, (n_sess, width)), "sess", 0, 0, tiled=True
    )
    query_all = lax.all_to_all(
        jnp.broadcast_to(queries, (n_tensor, queries.shape[1])), "tensor", 0, 0, tiled=True
    )

    down = adapter_down_maps.transpose(1, 0, 2, 3).reshape(two * slots * ranks, width)
    reduced = lax.dot_general(
        hidden_all, down, (((1,), (1,)), ((), ())), preferred_element_type=f32
    ).astype(bf16)
    slot_of_column = o * slots + jnp.arange(slots, dtype=jnp.int32)
    chosen = (session_slot[:, None] == slot_of_column[None, :])[:, None, :, None]
    reduced = jnp.where(
        chosen, reduced.reshape(n_sess, two, slots, ranks), jnp.zeros((), bf16)
    ).reshape(n_sess, two, slots * ranks)
    up = adapter_up_maps.transpose(1, 0, 2, 3).reshape(two, slots * ranks, kv_width)
    lifted = jnp.concatenate(
        [
            jnp.dot(reduced[:, k], up[k], preferred_element_type=f32)
            for k in range(two)
        ],
        axis=1,
    )
    partial = jnp.sum(
        lax.all_to_all(lifted, "sess", 0, 0, tiled=True), axis=0
    ).reshape(2 * KVH, HD)
    base = jnp.dot(hidden, key_value_weight, preferred_element_type=f32)
    blocks = jnp.arange(2 * KVH, dtype=jnp.int32)
    partial = partial * ADAPTER_SCALE + jnp.where(
        (blocks == t)[:, None], base.reshape(1, HD), 0.0
    )

    q = query_all.reshape(KVH, group, HD)
    k = cached_key_rows.reshape(span, KVH, HD)
    v = cached_value_rows.reshape(span, KVH, HD)
    positions = t * span + jnp.arange(span, dtype=jnp.int32)
    live = (positions < length)[None, None, :]
    scores = jnp.einsum("gjd,pgd->gjp", q, k, preferred_element_type=f32) * (
        1.0 / math.sqrt(HD)
    )
    scores = jnp.where(live, scores, MASKED)
    top = jnp.max(scores, axis=2)
    weights = jnp.where(live, jnp.exp(scores - top[..., None]), 0.0)
    total = jnp.sum(weights, axis=2)
    accum = jnp.einsum("gjp,pgd->gjd", weights.astype(bf16), v, preferred_element_type=f32)

    dest = jnp.arange(n_tensor, dtype=jnp.int32)
    outgoing = jnp.concatenate(
        [
            accum.reshape(n_tensor, own_heads, HD),
            jnp.broadcast_to(top.reshape(n_tensor, own_heads, 1), (n_tensor, own_heads, HD)),
            jnp.broadcast_to(total.reshape(n_tensor, own_heads, 1), (n_tensor, own_heads, HD)),
            partial[:, None],
            jnp.repeat(partial[:KVH], 2, axis=0)[:, None],
            jnp.repeat(partial[KVH:], 2, axis=0)[:, None],
            jnp.zeros((n_tensor, 1, HD), f32),
        ],
        axis=1,
    )
    incoming = lax.all_to_all(outgoing, "tensor", 0, 0, tiled=True)

    h = own_heads
    rows = jnp.sum(incoming[:, 3 * h : 3 * h + 3], axis=0)
    half = HD // 2
    inverse = jnp.exp(
        -(2.0 * jnp.arange(half, dtype=f32) / HD) * math.log(ROPE_BASE)
    )
    angles = length.astype(f32) * inverse
    cosine, sine = jnp.cos(angles), jnp.sin(angles)
    own = jnp.where(t < KVH, rotate_head(rows[0], cosine, sine), rows[0]).astype(bf16)
    new_key = rotate_head(rows[1], cosine, sine).astype(bf16)
    new_value = rows[2].astype(bf16)

    new_score = jnp.sum(
        queries.reshape(h, HD).astype(f32) * new_key.astype(f32)[None], axis=1
    ) * (1.0 / math.sqrt(HD))
    tops = incoming[:, h : 2 * h]
    new_score = jnp.broadcast_to(new_score[:, None], (h, HD))
    highest = jnp.maximum(jnp.max(tops, axis=0), new_score)
    factors = jnp.exp(tops - highest[None])
    new_weight = jnp.exp(new_score - highest)
    denom = jnp.sum(factors * incoming[:, 2 * h : 3 * h], axis=0) + new_weight
    summed = jnp.sum(factors * incoming[:, :h], axis=0) + new_weight.astype(bf16).astype(
        f32
    ) * new_value.astype(f32)[None]
    attended = (summed / denom).astype(bf16).reshape(1, h * HD)
    return (own.reshape(1, HD), attended)


def solution(mesh):
    return jax.shard_map(
        local,
        mesh=mesh,
        in_specs=(
            P("sess", None),
            P(None, "tensor"),
            P("sess", None, "tensor", None),
            P("sess", None, "tensor", None),
            P(),
            P("sess"),
            P("sess", "tensor"),
            P("sess", "tensor", None),
            P("sess", "tensor", None),
        ),
        out_specs=(P("sess", "tensor"), P("sess", "tensor")),
        check_vma=False,
    )
```

```python
import math

import jax
import jax.numpy as jnp
from jax import lax
from jax.experimental import pallas as pl
from jax.experimental.pallas import tpu as pltpu
from jax.sharding import PartitionSpec as P

QH = 64
KVH = 8
HD = 128
GROUP = QH // KVH
ADAPTER_SCALE = 0.5
ROPE_BASE = 500000.0
MASKED = -1e30
F32 = jnp.float32
BF16 = jnp.bfloat16

VMEM = pl.BlockSpec(memory_space=pltpu.VMEM)
SMEM = pl.BlockSpec(memory_space=pltpu.SMEM)


def call(body, out_shape, specs, args, cost):
    return pl.pallas_call(
        body,
        out_shape=out_shape,
        in_specs=specs,
        out_specs=jax.tree.map(lambda _: VMEM, out_shape),
        cost_estimate=pl.CostEstimate(flops=cost, bytes_accessed=cost, transcendentals=0),
        compiler_params=pltpu.CompilerParams(vmem_limit_bytes=24 * 1024 * 1024),
    )(*args)


def holder(slot_ref, slot, n_sess):
    index = jnp.int32(0)
    found = jnp.int32(0)
    for s in range(n_sess):
        hit = slot_ref[s] == slot
        index = jnp.where(hit, jnp.int32(s), index)
        found = jnp.where(hit, jnp.int32(1), found)
    return index, found


def spread_kernel(hidden_ref, out_ref):
    n, rows, lanes = out_ref.shape
    part = rows * lanes
    start = pl.multiple_of(lax.axis_index("tensor") * part, part)
    x = hidden_ref[:, pl.ds(start, part)].astype(F32)
    x = jnp.concatenate([x[:, j * lanes : (j + 1) * lanes] for j in range(rows)], axis=0)
    out_ref[...] = jnp.broadcast_to(x[None], out_ref.shape)


def select_kernel(slot_ref, arrived_ref, query_ref, out_ref):
    n_sess = arrived_ref.shape[0]
    o = lax.axis_index("sess")
    t = lax.axis_index("tensor")
    first, _ = holder(slot_ref, 2 * o, n_sess)
    second, _ = holder(slot_ref, 2 * o + 1, n_sess)
    q = query_ref[...].astype(F32)
    q = jnp.concatenate([q[:, j * HD : (j + 1) * HD] for j in range(4)], axis=0)
    even = jnp.bitwise_and(t, 1) == 0
    zero = jnp.zeros_like(q)
    block = jnp.concatenate(
        [
            jnp.where(even, q, zero),
            jnp.where(even, zero, q),
            arrived_ref[first],
            arrived_ref[second],
        ],
        axis=0,
    ).astype(BF16)
    out_ref[...] = jnp.broadcast_to(block[None], out_ref.shape)


def adapter_kernel(slot_ref, arrived_ref, down_ref, up_ref, out_ref):
    n_sess = out_ref.shape[0]
    n_tensor = arrived_ref.shape[0]
    ranks = down_ref.shape[0] // 2
    o = lax.axis_index("sess")
    x = arrived_ref[...].astype(F32)[:, 8:, :]
    upper = lax.broadcasted_iota(jnp.int32, (8, HD), 0) < 4
    reduced = [[], []]
    for row in range(2 * ranks):
        d = down_ref[row].astype(F32).reshape(n_tensor, 8, HD)
        total = jnp.sum(x * d, axis=0)
        for a in range(2):
            kept = jnp.where(upper if a == 0 else ~upper, total, 0.0)
            value = jnp.sum(jnp.sum(kept, axis=0, keepdims=True), axis=1, keepdims=True)
            reduced[a].append(value.astype(BF16).astype(F32))
    out_ref[...] = jnp.zeros(out_ref.shape, out_ref.dtype)
    for a in range(2):
        lifted = []
        for k in range(2):
            acc = None
            for r in range(ranks):
                term = reduced[a][k * ranks + r] * up_ref[(a * 2 + k) * ranks + r]
                acc = term if acc is None else acc + term
            lifted.append(acc)
        lifted = (jnp.concatenate(lifted, axis=0) * ADAPTER_SCALE).astype(out_ref.dtype)
        index, found = holder(slot_ref, 2 * o + a, n_sess)

        @pl.when(found == 1)
        def _():
            out_ref[index] = lifted


def attention_kernel(length_ref, arrived_ref, key_ref, value_ref, out_ref):
    span = key_ref.shape[1]
    t = lax.axis_index("tensor")
    length = length_ref[0]
    k = key_ref[0]
    v = value_ref[0]
    scores = []
    for g in range(KVH):
        q = (
            arrived_ref[2 * g].astype(F32)[:8] + arrived_ref[2 * g + 1].astype(F32)[:8]
        ).astype(BF16)
        scores.append(
            lax.dot_general(
                q,
                k[:, g * HD : (g + 1) * HD],
                (((1,), (1,)), ((), ())),
                preferred_element_type=F32,
            )
        )
    s = jnp.concatenate(scores, axis=0) * (1.0 / math.sqrt(HD))
    live = (t * span + lax.broadcasted_iota(jnp.int32, s.shape, 1)) < length
    s = jnp.where(live, s, MASKED)
    top = jnp.max(s, axis=1, keepdims=True)
    w = jnp.where(live, jnp.exp(s - top), 0.0)
    total = jnp.sum(w, axis=1, keepdims=True)
    wb = w.astype(BF16)
    lane = lax.broadcasted_iota(jnp.int32, (QH, HD), 1)
    head = jnp.bitwise_and(lax.broadcasted_iota(jnp.int32, (QH, HD), 0), 3)
    stats = jnp.where(lane == head, top, 0.0) + jnp.where(lane == head + 4, total, 0.0)
    zero = jnp.zeros((3, HD), F32)
    for g in range(KVH):
        acc = jnp.dot(
            wb[g * GROUP : (g + 1) * GROUP],
            v[:, g * HD : (g + 1) * HD],
            preferred_element_type=F32,
        )
        for half in range(2):
            rows = slice(4 * half, 4 * half + 4)
            stat = jnp.sum(stats[g * GROUP : (g + 1) * GROUP][rows], axis=0, keepdims=True)
            out_ref[2 * g + half] = jnp.concatenate([acc[rows], zero, stat], axis=0)


def pack_kernel(slot_ref, arrived_ref, base_ref, partial_ref, out_ref):
    s = lax.axis_index("sess")
    t = lax.axis_index("tensor")
    owner = lax.shift_right_logical(slot_ref[s], 1)
    row = lax.broadcasted_iota(jnp.int32, (2 * KVH, HD), 0)
    p = arrived_ref[owner].astype(F32) + jnp.where(row == t, base_ref[...], 0.0)
    out_ref[...] = partial_ref[...]
    for d in range(out_ref.shape[0]):
        g = d // 2
        out_ref[d, 4:7, :] = jnp.concatenate(
            [p[d : d + 1], p[g : g + 1], p[KVH + g : KVH + g + 1]], axis=0
        )


def merge_kernel(rot_ref, query_ref, arrived_ref, fresh_ref, attended_ref):
    r = arrived_ref[...]
    n = r.shape[0]
    sums = jnp.sum(r, axis=0)
    own, key, value = sums[4:5], sums[5:6], sums[6:7]
    half = HD // 2
    own = own * rot_ref[2:3] + pltpu.roll(own, half, 1) * rot_ref[3:4]
    key = key * rot_ref[0:1] + pltpu.roll(key, half, 1) * rot_ref[1:2]
    fresh_ref[...] = own.astype(BF16)
    key = key.astype(BF16).astype(F32)
    value = value.astype(BF16).astype(F32)
    q = query_ref[...].astype(F32)
    q = jnp.concatenate([q[:, j * HD : (j + 1) * HD] for j in range(4)], axis=0)
    new_score = jnp.sum(q * key, axis=1, keepdims=True) * (1.0 / math.sqrt(HD))
    shape = (n, 8, HD)
    picked = lax.broadcasted_iota(jnp.int32, shape, 1) == lax.broadcasted_iota(
        jnp.int32, shape, 2
    )
    stats = jnp.sum(
        jnp.where(picked, jnp.broadcast_to(r[:, 7:8, :], shape), 0.0), axis=2, keepdims=True
    )
    tops, totals = stats[:, :4], stats[:, 4:]
    highest = jnp.maximum(jnp.max(tops, axis=0), new_score)
    factors = jnp.exp(tops - highest[None])
    weight = jnp.exp(new_score - highest)
    denom = jnp.sum(factors * totals, axis=0) + weight
    summed = jnp.sum(factors * r[:, :4, :], axis=0) + weight.astype(BF16).astype(F32) * value
    result = (summed / denom).astype(BF16).astype(F32)
    for j in range(4):
        attended_ref[:, j * HD : (j + 1) * HD] = result[j : j + 1].astype(BF16)


def local(
    hidden,
    key_value_weight,
    adapter_down_maps,
    adapter_up_maps,
    session_slot,
    lengths,
    queries,
    cached_key_rows,
    cached_value_rows,
):
    n_sess = lax.axis_size("sess")
    n_tensor = lax.axis_size("tensor")
    t = lax.axis_index("tensor")
    slots, two, ranks, width = adapter_down_maps.shape
    part = width // n_tensor // HD
    shape = jax.ShapeDtypeStruct

    parts = call(spread_kernel, shape((n_sess, part, HD), F32), [VMEM], [hidden], 10**5)
    parts = lax.all_to_all(parts, "sess", 0, 0, tiled=True)

    block = call(
        select_kernel,
        shape((n_tensor, 16, HD), BF16),
        [SMEM, VMEM, VMEM],
        [session_slot, parts, queries],
        10**5,
    )
    block = lax.all_to_all(block, "tensor", 0, 0, tiled=True)

    down = (
        adapter_down_maps.reshape(slots, two, ranks, n_tensor, part, HD)
        .transpose(1, 2, 3, 0, 4, 5)
        .reshape(two * ranks, n_tensor * slots * part, HD)
    )
    up = adapter_up_maps.reshape(slots * two * ranks, KVH, HD).astype(F32)
    terms = call(
        adapter_kernel,
        shape((n_sess, 2 * KVH, HD), BF16),
        [SMEM, VMEM, VMEM, VMEM],
        [session_slot, block, down, up],
        10**6,
    )
    terms = lax.all_to_all(terms, "sess", 0, 0, tiled=True)

    partial = call(
        attention_kernel,
        shape((n_tensor, 8, HD), F32),
        [SMEM, VMEM, VMEM, VMEM],
        [lengths, block, cached_key_rows, cached_value_rows],
        10**7,
    )
    base = jnp.dot(hidden, key_value_weight, preferred_element_type=F32)
    packed = call(
        pack_kernel,
        shape((n_tensor, 8, HD), F32),
        [SMEM, VMEM, VMEM, VMEM],
        [session_slot, terms, base, partial],
        10**5,
    )
    packed = lax.all_to_all(packed, "tensor", 0, 0, tiled=True)

    half = HD // 2
    inverse = jnp.exp(-(2.0 * jnp.arange(half, dtype=F32) / HD) * math.log(ROPE_BASE))
    angles = lengths[0].astype(F32) * inverse
    cosine, sine = jnp.cos(angles), jnp.sin(angles)
    cosine = jnp.concatenate([cosine, cosine])
    sine = jnp.concatenate([-sine, sine])
    keyed = t < KVH
    rot = jnp.stack(
        [cosine, sine, jnp.where(keyed, cosine, 1.0), jnp.where(keyed, sine, 0.0)]
    )
    return call(
        merge_kernel,
        (shape((1, HD), BF16), shape((1, 4 * HD), BF16)),
        [VMEM, VMEM, VMEM],
        [rot, queries, packed],
        10**5,
    )


def solution(mesh):
    return jax.shard_map(
        local,
        mesh=mesh,
        in_specs=(
            P("sess", None),
            P(None, "tensor"),
            P("sess", None, "tensor", None),
            P("sess", None, "tensor", None),
            P(),
            P("sess"),
            P("sess", "tensor"),
            P("sess", "tensor", None),
            P("sess", "tensor", None),
        ),
        out_specs=(P("sess", "tensor"), P("sess", "tensor")),
        check_vma=False,
    )
```

```python
import math

import jax
import jax.numpy as jnp
from jax import lax
from jax.experimental import pallas as pl
from jax.experimental.pallas import tpu as pltpu
from jax.sharding import PartitionSpec as P

QH = 64
KVH = 8
HD = 128
GROUP = QH // KVH
ADAPTER_SCALE = 0.5
ROPE_BASE = 500000.0
MASKED = -1e30
F32 = jnp.float32
BF16 = jnp.bfloat16

VMEM = pl.BlockSpec(memory_space=pltpu.VMEM)
SMEM = pl.BlockSpec(memory_space=pltpu.SMEM)
HBM = pl.BlockSpec(memory_space=pltpu.HBM)


def call(body, out_shape, specs, args, cost):
    return pl.pallas_call(
        body,
        out_shape=out_shape,
        in_specs=specs,
        out_specs=jax.tree.map(
            lambda x: SMEM if getattr(x, "memory_space", None) == pltpu.SMEM else VMEM, out_shape
        ),
        cost_estimate=pl.CostEstimate(flops=cost, bytes_accessed=cost, transcendentals=0),
        compiler_params=pltpu.CompilerParams(vmem_limit_bytes=24 * 1024 * 1024),
    )(*args)


def holder(slot_ref, slot, n_sess):
    index = jnp.int32(0)
    found = jnp.int32(0)
    for s in range(n_sess):
        hit = slot_ref[s] == slot
        index = jnp.where(hit, jnp.int32(s), index)
        found = jnp.where(hit, jnp.int32(1), found)
    return index, found


def spread_kernel(
    slot_hbm, hidden_hbm, query_hbm, out_hbm, query_out, index_ref, slot, hidden, query, chunks, sem, out_sem
):
    copies = [
        pltpu.make_async_copy(hidden_hbm, hidden, sem.at[0]),
        pltpu.make_async_copy(query_hbm, query, sem.at[1]),
        pltpu.make_async_copy(slot_hbm, slot, sem.at[2]),
    ]
    for copy in copies:
        copy.start()
    n_sess, rows, lanes = out_hbm.shape
    o = lax.axis_index("sess")
    t = lax.axis_index("tensor")
    copies[0].wait()
    x = hidden[...].astype(F32)
    x = jnp.concatenate([x[:, j * lanes : (j + 1) * lanes] for j in range(rows)], axis=0)
    x = x.astype(BF16)
    sends = []
    step = n_sess // 4
    for s in range(4):
        places = pl.ds(s * step, step)
        chunks[places] = jnp.broadcast_to(x[None], (step, rows, lanes))
        sends.append(pltpu.make_async_copy(chunks.at[places], out_hbm.at[places], out_sem.at[s]))
        sends[-1].start()
    copies[1].wait()
    q = query[...].astype(F32)
    q = jnp.concatenate([q[:, j * HD : (j + 1) * HD] for j in range(4)], axis=0)
    even = jnp.bitwise_and(t, 1) == 0
    zero = jnp.zeros_like(q)
    query_out[...] = jnp.concatenate(
        [jnp.where(even, q, zero), jnp.where(even, zero, q)], axis=0
    )
    copies[2].wait()
    for a in range(2):
        index, found = holder(slot, 2 * o + a, n_sess)
        index_ref[2 * a] = index
        index_ref[2 * a + 1] = found
    index_ref[4] = lax.shift_right_logical(slot[o], 1)
    for send in sends:
        send.wait()


def adapter_kernel(index_ref, arrived_ref, down_ref, up_ref, out_ref, mark_ref):
    ranks = down_ref.shape[2]
    rows, lanes = arrived_ref.shape[1:]
    mark_ref[0] = jnp.int32(0)
    out_ref[...] = jnp.zeros(out_ref.shape, out_ref.dtype)
    for a in range(2):
        index = index_ref[2 * a]
        x = arrived_ref[index].astype(F32)
        heads = []
        for k in range(2):
            d = down_ref[a, k].astype(F32)
            acc = None
            for i in range(rows):
                term = d[:, i * lanes : (i + 1) * lanes] * x[i : i + 1]
                acc = term if acc is None else acc + term
            reduced = jnp.sum(acc, axis=1, keepdims=True).astype(BF16).astype(F32)
            lifted = jnp.sum(reduced * up_ref[a, k].astype(F32), axis=0, keepdims=True)
            heads += [lifted[:, h * HD : (h + 1) * HD] for h in range(KVH)]
        lifted = (jnp.concatenate(heads, axis=0) * ADAPTER_SCALE).astype(out_ref.dtype)

        @pl.when(index_ref[2 * a + 1] == 1)
        def _():
            out_ref[index] = lifted


def attention_kernel(
    length_ref, mark_ref, before_ref, spread_ref, after_ref, key_ref, value_ref, out_ref
):
    span = key_ref.shape[1]
    t = lax.axis_index("tensor")
    length = length_ref[0]
    k = key_ref[0]
    v = value_ref[0]
    scores = []
    for g in range(KVH):
        place = jnp.bitwise_and(g - lax.shift_right_logical(t, 1) + 4, 7)
        row = lax.shift_right_logical(place * 11, 5)
        part = place - 3 * row
        q = jnp.where(
            part == 0,
            before_ref[row],
            jnp.where(part == 1, spread_ref[row], after_ref[row]),
        ).astype(BF16)
        scores.append(
            lax.dot_general(
                q,
                k[:, g * HD : (g + 1) * HD],
                (((1,), (1,)), ((), ())),
                preferred_element_type=F32,
            )
        )
    s = jnp.concatenate(scores, axis=0) * (1.0 / math.sqrt(HD))
    live = (t * span + lax.broadcasted_iota(jnp.int32, s.shape, 1)) < length
    s = jnp.where(live, s, MASKED)
    top = jnp.max(s, axis=1, keepdims=True)
    w = jnp.where(live, jnp.exp(s - top), 0.0)
    total = jnp.sum(w, axis=1, keepdims=True)
    wb = w.astype(BF16)
    lane = lax.broadcasted_iota(jnp.int32, (QH, HD), 1)
    head = jnp.bitwise_and(lax.broadcasted_iota(jnp.int32, (QH, HD), 0), 3)
    stats = jnp.where(lane == head, top, 0.0) + jnp.where(lane == head + 4, total, 0.0)
    zero = jnp.zeros((3, HD), F32)
    for g in range(KVH):
        acc = jnp.dot(
            wb[g * GROUP : (g + 1) * GROUP],
            v[:, g * HD : (g + 1) * HD],
            preferred_element_type=F32,
        )
        for half in range(2):
            rows = slice(4 * half, 4 * half + 4)
            stat = jnp.sum(stats[g * GROUP : (g + 1) * GROUP][rows], axis=0, keepdims=True)
            out_ref[2 * g + half] = jnp.concatenate([acc[rows], zero, stat], axis=0)


def pack_kernel(index_ref, arrived_ref, base_ref, partial_ref, out_ref):
    t = lax.axis_index("tensor")
    owner = index_ref[4]
    row = lax.broadcasted_iota(jnp.int32, (2 * KVH, HD), 0)
    p = arrived_ref[owner].astype(F32) + jnp.where(row == t, base_ref[...], 0.0)
    out_ref[...] = partial_ref[...]
    for d in range(out_ref.shape[0]):
        g = d // 2
        out_ref[d, 4:7, :] = jnp.concatenate(
            [p[d : d + 1], p[g : g + 1], p[KVH + g : KVH + g + 1]], axis=0
        )


def merge_kernel(rot_ref, query_ref, arrived_ref, fresh_ref, attended_ref):
    r = arrived_ref[...]
    n = r.shape[0]
    sums = jnp.sum(r, axis=0)
    own, key, value = sums[4:5], sums[5:6], sums[6:7]
    half = HD // 2
    own = own * rot_ref[2:3] + pltpu.roll(own, half, 1) * rot_ref[3:4]
    key = key * rot_ref[0:1] + pltpu.roll(key, half, 1) * rot_ref[1:2]
    fresh_ref[...] = own.astype(BF16)
    key = key.astype(BF16).astype(F32)
    value = value.astype(BF16).astype(F32)
    q = query_ref[...].astype(F32)
    q = jnp.concatenate([q[:, j * HD : (j + 1) * HD] for j in range(4)], axis=0)
    new_score = jnp.sum(q * key, axis=1, keepdims=True) * (1.0 / math.sqrt(HD))
    shape = (n, 8, HD)
    picked = lax.broadcasted_iota(jnp.int32, shape, 1) == lax.broadcasted_iota(
        jnp.int32, shape, 2
    )
    stats = jnp.sum(
        jnp.where(picked, jnp.broadcast_to(r[:, 7:8, :], shape), 0.0), axis=2, keepdims=True
    )
    tops, totals = stats[:, :4], stats[:, 4:]
    highest = jnp.maximum(jnp.max(tops, axis=0), new_score)
    factors = jnp.exp(tops - highest[None])
    weight = jnp.exp(new_score - highest)
    denom = jnp.sum(factors * totals, axis=0) + weight
    summed = jnp.sum(factors * r[:, :4, :], axis=0) + weight.astype(BF16).astype(F32) * value
    result = (summed / denom).astype(BF16).astype(F32)
    for j in range(4):
        attended_ref[:, j * HD : (j + 1) * HD] = result[j : j + 1].astype(BF16)


def local(
    hidden,
    key_value_weight,
    adapter_down_maps,
    adapter_up_maps,
    session_slot,
    lengths,
    queries,
    cached_key_rows,
    cached_value_rows,
):
    n_sess = lax.axis_size("sess")
    n_tensor = lax.axis_size("tensor")
    t = lax.axis_index("tensor")
    slots, two, ranks, width = adapter_down_maps.shape
    shape = jax.ShapeDtypeStruct

    parts, own_queries, index = pl.pallas_call(
        spread_kernel,
        out_shape=(
            pltpu.HBM((n_sess, 16, width // 16), BF16),
            shape((8, HD), F32),
            pltpu.SMEM((8,), jnp.int32),
        ),
        in_specs=[HBM, HBM, HBM],
        out_specs=(HBM, VMEM, SMEM),
        scratch_shapes=[
            pltpu.SMEM((n_sess,), jnp.int32),
            pltpu.VMEM(hidden.shape, BF16),
            pltpu.VMEM(queries.shape, BF16),
            pltpu.VMEM((n_sess, 16, width // 16), BF16),
            pltpu.SemaphoreType.DMA((3,)),
            pltpu.SemaphoreType.DMA((4,)),
        ],
        cost_estimate=pl.CostEstimate(flops=10**5, bytes_accessed=10**5, transcendentals=0),
        compiler_params=pltpu.CompilerParams(vmem_limit_bytes=24 * 1024 * 1024),
    )(*(pltpu.with_memory_space_constraint(x, pltpu.HBM) for x in (session_slot, hidden, queries)))
    parts = lax.all_to_all(parts, "sess", 0, 0, tiled=True)

    def come(x, distance):
        return lax.ppermute(
            x, "tensor", [(i, (i - 2 * distance) % n_tensor) for i in range(n_tensor)]
        )

    pair = own_queries + lax.ppermute(
        own_queries, "tensor", [(i, i ^ 1) for i in range(n_tensor)]
    )
    pair = pair[None]
    spread = jnp.concatenate([come(pair, -3), pair, come(pair, 3)])
    before, after = come(spread, -1), come(spread, 1)

    terms, mark = call(
        adapter_kernel,
        (shape((n_sess, 2 * KVH, HD), BF16), pltpu.SMEM((8,), jnp.int32)),
        [SMEM, VMEM, VMEM, VMEM],
        [index, parts, adapter_down_maps, adapter_up_maps],
        10**6,
    )
    terms = lax.all_to_all(terms, "sess", 0, 0, tiled=True)

    partial = call(
        attention_kernel,
        shape((n_tensor, 8, HD), F32),
        [SMEM, SMEM, VMEM, VMEM, VMEM, VMEM, VMEM],
        [lengths, mark, before, spread, after, cached_key_rows, cached_value_rows],
        10**7,
    )
    base = jnp.dot(hidden, key_value_weight, preferred_element_type=F32)
    packed = call(
        pack_kernel,
        shape((n_tensor, 8, HD), F32),
        [SMEM, VMEM, VMEM, VMEM],
        [index, terms, base, partial],
        10**5,
    )
    packed = lax.all_to_all(packed, "tensor", 0, 0, tiled=True)

    half = HD // 2
    inverse = jnp.exp(-(2.0 * jnp.arange(half, dtype=F32) / HD) * math.log(ROPE_BASE))
    angles = lengths[0].astype(F32) * inverse
    cosine, sine = jnp.cos(angles), jnp.sin(angles)
    cosine = jnp.concatenate([cosine, cosine])
    sine = jnp.concatenate([-sine, sine])
    keyed = t < KVH
    rot = jnp.stack(
        [cosine, sine, jnp.where(keyed, cosine, 1.0), jnp.where(keyed, sine, 0.0)]
    )
    return call(
        merge_kernel,
        (shape((1, HD), BF16), shape((1, 4 * HD), BF16)),
        [VMEM, VMEM, VMEM],
        [rot, queries, packed],
        10**5,
    )


def solution(mesh):
    return jax.shard_map(
        local,
        mesh=mesh,
        in_specs=(
            P("sess", None),
            P(None, "tensor"),
            P("sess", None, "tensor", None),
            P("sess", None, "tensor", None),
            P(),
            P("sess"),
            P("sess", "tensor"),
            P("sess", "tensor", None),
            P("sess", "tensor", None),
        ),
        out_specs=(P("sess", "tensor"), P("sess", "tensor")),
        check_vma=False,
    )
```

```python
import math

import jax
import jax.numpy as jnp
from jax import lax
from jax.experimental import pallas as pl
from jax.experimental.pallas import tpu as pltpu
from jax.sharding import PartitionSpec as P

QH = 64
KVH = 8
HD = 128
GROUP = QH // KVH
ADAPTER_SCALE = 0.5
ROPE_BASE = 500000.0
MASKED = -1e30
F32 = jnp.float32
BF16 = jnp.bfloat16

VMEM = pl.BlockSpec(memory_space=pltpu.VMEM)
SMEM = pl.BlockSpec(memory_space=pltpu.SMEM)
HBM = pl.BlockSpec(memory_space=pltpu.HBM)


def call(body, out_shape, specs, args, cost):
    return pl.pallas_call(
        body,
        out_shape=out_shape,
        in_specs=specs,
        out_specs=jax.tree.map(
            lambda x: SMEM if getattr(x, "memory_space", None) == pltpu.SMEM else VMEM, out_shape
        ),
        cost_estimate=pl.CostEstimate(flops=cost, bytes_accessed=cost, transcendentals=0),
        compiler_params=pltpu.CompilerParams(vmem_limit_bytes=24 * 1024 * 1024),
    )(*args)


def holder(slot_ref, slot, n_sess):
    index = jnp.int32(0)
    found = jnp.int32(0)
    for s in range(n_sess):
        hit = slot_ref[s] == slot
        index = jnp.where(hit, jnp.int32(s), index)
        found = jnp.where(hit, jnp.int32(1), found)
    return index, found


def spread_kernel(
    slot_hbm, hidden_hbm, query_hbm, out_hbm, query_out, index_ref, slot, hidden, query, chunks, sem, out_sem
):
    copies = [
        pltpu.make_async_copy(hidden_hbm, hidden, sem.at[0]),
        pltpu.make_async_copy(query_hbm, query, sem.at[1]),
        pltpu.make_async_copy(slot_hbm, slot, sem.at[2]),
    ]
    for copy in copies:
        copy.start()
    n_sess, rows, lanes = out_hbm.shape
    o = lax.axis_index("sess")
    t = lax.axis_index("tensor")
    copies[0].wait()
    x = hidden[...].astype(F32)
    x = jnp.concatenate([x[:, j * lanes : (j + 1) * lanes] for j in range(rows)], axis=0)
    x = x.astype(BF16)
    sends = []
    step = n_sess // 4
    for s in range(4):
        places = pl.ds(s * step, step)
        chunks[places] = jnp.broadcast_to(x[None], (step, rows, lanes))
        sends.append(pltpu.make_async_copy(chunks.at[places], out_hbm.at[places], out_sem.at[s]))
        sends[-1].start()
    copies[1].wait()
    q = query[...].astype(F32)
    q = jnp.concatenate([q[:, j * HD : (j + 1) * HD] for j in range(4)], axis=0)
    even = jnp.bitwise_and(t, 1) == 0
    zero = jnp.zeros_like(q)
    query_out[...] = jnp.concatenate(
        [jnp.where(even, q, zero), jnp.where(even, zero, q)], axis=0
    )
    copies[2].wait()
    for a in range(2):
        index, found = holder(slot, 2 * o + a, n_sess)
        index_ref[2 * a] = index
        index_ref[2 * a + 1] = found
    index_ref[4] = lax.shift_right_logical(slot[o], 1)
    for send in sends:
        send.wait()


def adapter_kernel(index_ref, arrived_ref, down_ref, up_ref, out_ref, mark_ref):
    ranks = down_ref.shape[2]
    rows, lanes = arrived_ref.shape[1:]
    mark_ref[0] = jnp.int32(0)
    out_ref[...] = jnp.zeros(out_ref.shape, out_ref.dtype)
    for a in range(2):
        index = index_ref[2 * a]
        x = arrived_ref[index].astype(F32)
        heads = []
        for k in range(2):
            d = down_ref[a, k].astype(F32)
            acc = None
            for i in range(rows):
                term = d[:, i * lanes : (i + 1) * lanes] * x[i : i + 1]
                acc = term if acc is None else acc + term
            reduced = jnp.sum(acc, axis=1, keepdims=True).astype(BF16).astype(F32)
            lifted = jnp.sum(reduced * up_ref[a, k].astype(F32), axis=0, keepdims=True)
            heads += [lifted[:, h * HD : (h + 1) * HD] for h in range(KVH)]
        lifted = (jnp.concatenate(heads, axis=0) * ADAPTER_SCALE).astype(out_ref.dtype)

        @pl.when(index_ref[2 * a + 1] == 1)
        def _():
            out_ref[index] = lifted


def attention_kernel(
    length_ref, mark_ref, before_ref, spread_ref, after_ref, key_ref, value_ref, out_ref
):
    span = key_ref.shape[1]
    t = lax.axis_index("tensor")
    length = length_ref[0]
    k = key_ref[0]
    v = value_ref[0]
    scores = []
    for g in range(KVH):
        place = jnp.bitwise_and(g - lax.shift_right_logical(t, 1) + 4, 7)
        row = lax.shift_right_logical(place * 11, 5)
        part = place - 3 * row
        q = jnp.where(
            part == 0,
            before_ref[row],
            jnp.where(part == 1, spread_ref[row], after_ref[row]),
        ).astype(BF16)
        scores.append(
            lax.dot_general(
                q,
                k[:, g * HD : (g + 1) * HD],
                (((1,), (1,)), ((), ())),
                preferred_element_type=F32,
            )
        )
    s = jnp.concatenate(scores, axis=0) * (1.0 / math.sqrt(HD))
    live = (t * span + lax.broadcasted_iota(jnp.int32, s.shape, 1)) < length
    s = jnp.where(live, s, MASKED)
    top = jnp.max(s, axis=1, keepdims=True)
    w = jnp.where(live, jnp.exp(s - top), 0.0)
    total = jnp.sum(w, axis=1, keepdims=True)
    wb = w.astype(BF16)
    lane = lax.broadcasted_iota(jnp.int32, (QH, HD), 1)
    head = jnp.bitwise_and(lax.broadcasted_iota(jnp.int32, (QH, HD), 0), 3)
    stats = jnp.where(lane == head, top, 0.0) + jnp.where(lane == head + 4, total, 0.0)
    zero = jnp.zeros((3, HD), F32)
    for g in range(KVH):
        acc = jnp.dot(
            wb[g * GROUP : (g + 1) * GROUP],
            v[:, g * HD : (g + 1) * HD],
            preferred_element_type=F32,
        )
        for half in range(2):
            rows = slice(4 * half, 4 * half + 4)
            stat = jnp.sum(stats[g * GROUP : (g + 1) * GROUP][rows], axis=0, keepdims=True)
            out_ref[2 * g + half] = jnp.concatenate([acc[rows], zero, stat], axis=0)


def pack_kernel(index_ref, arrived_ref, base_ref, partial_ref, out_ref):
    t = lax.axis_index("tensor")
    owner = index_ref[4]
    row = lax.broadcasted_iota(jnp.int32, (2 * KVH, HD), 0)
    p = arrived_ref[owner].astype(F32) + jnp.where(row == t, base_ref[...], 0.0)
    out_ref[...] = partial_ref[...]
    for d in range(out_ref.shape[0]):
        g = d // 2
        out_ref[d, 4:7, :] = jnp.concatenate(
            [p[d : d + 1], p[g : g + 1], p[KVH + g : KVH + g + 1]], axis=0
        )


def merge_kernel(rot_ref, query_ref, arrived_ref, fresh_ref, attended_ref):
    r = arrived_ref[...]
    n = r.shape[0]
    sums = jnp.sum(r, axis=0)
    own, key, value = sums[4:5], sums[5:6], sums[6:7]
    half = HD // 2
    own = own * rot_ref[2:3] + pltpu.roll(own, half, 1) * rot_ref[3:4]
    key = key * rot_ref[0:1] + pltpu.roll(key, half, 1) * rot_ref[1:2]
    fresh_ref[...] = own.astype(BF16)
    key = key.astype(BF16).astype(F32)
    value = value.astype(BF16).astype(F32)
    q = query_ref[...].astype(F32)
    q = jnp.concatenate([q[:, j * HD : (j + 1) * HD] for j in range(4)], axis=0)
    new_score = jnp.sum(q * key, axis=1, keepdims=True) * (1.0 / math.sqrt(HD))
    shape = (n, 8, HD)
    picked = lax.broadcasted_iota(jnp.int32, shape, 1) == lax.broadcasted_iota(
        jnp.int32, shape, 2
    )
    stats = jnp.sum(
        jnp.where(picked, jnp.broadcast_to(r[:, 7:8, :], shape), 0.0), axis=2, keepdims=True
    )
    tops, totals = stats[:, :4], stats[:, 4:]
    highest = jnp.maximum(jnp.max(tops, axis=0), new_score)
    factors = jnp.exp(tops - highest[None])
    weight = jnp.exp(new_score - highest)
    denom = jnp.sum(factors * totals, axis=0) + weight
    summed = jnp.sum(factors * r[:, :4, :], axis=0) + weight.astype(BF16).astype(F32) * value
    result = (summed / denom).astype(BF16).astype(F32)
    for j in range(4):
        attended_ref[:, j * HD : (j + 1) * HD] = result[j : j + 1].astype(BF16)


def local(
    hidden,
    key_value_weight,
    adapter_down_maps,
    adapter_up_maps,
    session_slot,
    lengths,
    queries,
    cached_key_rows,
    cached_value_rows,
):
    n_sess = lax.axis_size("sess")
    n_tensor = lax.axis_size("tensor")
    t = lax.axis_index("tensor")
    slots, two, ranks, width = adapter_down_maps.shape
    shape = jax.ShapeDtypeStruct

    parts, own_queries, index = pl.pallas_call(
        spread_kernel,
        out_shape=(
            pltpu.HBM((n_sess, 16, width // 16), BF16),
            shape((8, HD), F32),
            pltpu.SMEM((8,), jnp.int32),
        ),
        in_specs=[HBM, HBM, HBM],
        out_specs=(HBM, VMEM, SMEM),
        scratch_shapes=[
            pltpu.SMEM((n_sess,), jnp.int32),
            pltpu.VMEM(hidden.shape, BF16),
            pltpu.VMEM(queries.shape, BF16),
            pltpu.VMEM((n_sess, 16, width // 16), BF16),
            pltpu.SemaphoreType.DMA((3,)),
            pltpu.SemaphoreType.DMA((4,)),
        ],
        cost_estimate=pl.CostEstimate(flops=10**5, bytes_accessed=10**5, transcendentals=0),
        compiler_params=pltpu.CompilerParams(vmem_limit_bytes=24 * 1024 * 1024),
    )(*(pltpu.with_memory_space_constraint(x, pltpu.HBM) for x in (session_slot, hidden, queries)))
    parts = lax.all_to_all(parts, "sess", 0, 0, tiled=True)

    def come(x, distance):
        return lax.ppermute(
            x, "tensor", [(i, (i - 2 * distance) % n_tensor) for i in range(n_tensor)]
        )

    pair = own_queries + lax.ppermute(
        own_queries, "tensor", [(i, i ^ 1) for i in range(n_tensor)]
    )
    pair = pair[None]
    spread = jnp.concatenate([come(pair, -3), pair, come(pair, 3)])
    before, after = come(spread, -1), come(spread, 1)

    terms, mark = call(
        adapter_kernel,
        (shape((n_sess, 2 * KVH, HD), F32), pltpu.SMEM((8,), jnp.int32)),
        [SMEM, VMEM, VMEM, VMEM],
        [index, parts, adapter_down_maps, adapter_up_maps],
        10**6,
    )
    terms = lax.all_to_all(terms, "sess", 0, 0, tiled=True)

    partial = call(
        attention_kernel,
        shape((n_tensor, 8, HD), F32),
        [SMEM, SMEM, VMEM, VMEM, VMEM, VMEM, VMEM],
        [lengths, mark, before, spread, after, cached_key_rows, cached_value_rows],
        10**7,
    )
    base = jnp.dot(hidden, key_value_weight, preferred_element_type=F32)
    packed = call(
        pack_kernel,
        shape((n_tensor, 8, HD), F32),
        [SMEM, VMEM, VMEM, VMEM],
        [index, terms, base, partial],
        10**5,
    )
    packed = lax.all_to_all(packed, "tensor", 0, 0, tiled=True)

    half = HD // 2
    inverse = jnp.exp(-(2.0 * jnp.arange(half, dtype=F32) / HD) * math.log(ROPE_BASE))
    angles = lengths[0].astype(F32) * inverse
    cosine, sine = jnp.cos(angles), jnp.sin(angles)
    cosine = jnp.concatenate([cosine, cosine])
    sine = jnp.concatenate([-sine, sine])
    keyed = t < KVH
    rot = jnp.stack(
        [cosine, sine, jnp.where(keyed, cosine, 1.0), jnp.where(keyed, sine, 0.0)]
    )
    return call(
        merge_kernel,
        (shape((1, HD), BF16), shape((1, 4 * HD), BF16)),
        [VMEM, VMEM, VMEM],
        [rot, queries, packed],
        10**5,
    )


def solution(mesh):
    return jax.shard_map(
        local,
        mesh=mesh,
        in_specs=(
            P("sess", None),
            P(None, "tensor"),
            P("sess", None, "tensor", None),
            P("sess", None, "tensor", None),
            P(),
            P("sess"),
            P("sess", "tensor"),
            P("sess", "tensor", None),
            P("sess", "tensor", None),
        ),
        out_specs=(P("sess", "tensor"), P("sess", "tensor")),
        check_vma=False,
    )
```

```python
import math

import jax
import jax.numpy as jnp
from jax import lax
from jax.experimental import pallas as pl
from jax.experimental.pallas import tpu as pltpu
from jax.sharding import PartitionSpec as P

QH = 64
KVH = 8
HD = 128
GROUP = QH // KVH
ADAPTER_SCALE = 0.5
ROPE_BASE = 500000.0
MASKED = -1e30
F32 = jnp.float32
BF16 = jnp.bfloat16

VMEM = pl.BlockSpec(memory_space=pltpu.VMEM)
SMEM = pl.BlockSpec(memory_space=pltpu.SMEM)
HBM = pl.BlockSpec(memory_space=pltpu.HBM)
ANY = pl.BlockSpec(memory_space=pl.ANY)


def call(body, out_shape, specs, args, cost):
    return pl.pallas_call(
        body,
        out_shape=out_shape,
        in_specs=specs,
        out_specs=jax.tree.map(
            lambda x: SMEM if getattr(x, "memory_space", None) == pltpu.SMEM else VMEM, out_shape
        ),
        cost_estimate=pl.CostEstimate(flops=cost, bytes_accessed=cost, transcendentals=0),
        compiler_params=pltpu.CompilerParams(vmem_limit_bytes=24 * 1024 * 1024),
    )(*args)


def holder(slot_ref, slot, n_sess):
    index = jnp.int32(0)
    found = jnp.int32(0)
    for s in range(n_sess):
        hit = slot_ref[s] == slot
        index = jnp.where(hit, jnp.int32(s), index)
        found = jnp.where(hit, jnp.int32(1), found)
    return index, found


def spread_kernel(
    slot_hbm,
    hidden_hbm,
    query_hbm,
    down_hbm,
    up_hbm,
    out_hbm,
    query_out,
    index_ref,
    down_out,
    up_out,
    slot,
    hidden,
    query,
    chunks,
    sem,
    out_sem,
):
    copies = [
        pltpu.make_async_copy(hidden_hbm, hidden, sem.at[0]),
        pltpu.make_async_copy(query_hbm, query, sem.at[1]),
        pltpu.make_async_copy(slot_hbm, slot, sem.at[2]),
        pltpu.make_async_copy(down_hbm, down_out, sem.at[3]),
        pltpu.make_async_copy(up_hbm, up_out, sem.at[4]),
    ]
    for copy in copies:
        copy.start()
    n_sess, rows, lanes = out_hbm.shape
    o = lax.axis_index("sess")
    t = lax.axis_index("tensor")
    copies[0].wait()
    x = hidden[...].astype(F32)
    x = jnp.concatenate([x[:, j * lanes : (j + 1) * lanes] for j in range(rows)], axis=0)
    x = x.astype(BF16)
    sends = []
    step = n_sess // 4
    for s in range(4):
        places = pl.ds(s * step, step)
        chunks[places] = jnp.broadcast_to(x[None], (step, rows, lanes))
        sends.append(pltpu.make_async_copy(chunks.at[places], out_hbm.at[places], out_sem.at[s]))
        sends[-1].start()
    copies[1].wait()
    q = query[...].astype(F32)
    q = jnp.concatenate([q[:, j * HD : (j + 1) * HD] for j in range(4)], axis=0)
    even = jnp.bitwise_and(t, 1) == 0
    zero = jnp.zeros_like(q)
    query_out[...] = jnp.concatenate(
        [jnp.where(even, q, zero), jnp.where(even, zero, q)], axis=0
    )
    copies[2].wait()
    for a in range(2):
        index, found = holder(slot, 2 * o + a, n_sess)
        index_ref[2 * a] = index
        index_ref[2 * a + 1] = found
    index_ref[4] = lax.shift_right_logical(slot[o], 1)
    copies[3].wait()
    copies[4].wait()
    for send in sends:
        send.wait()


def adapter_kernel(index_ref, arrived_ref, down_ref, up_ref, spread_ref, out_ref, mark_ref):
    ranks = down_ref.shape[2]
    rows, lanes = arrived_ref.shape[1:]
    mark_ref[0] = jnp.int32(0)
    out_ref[...] = jnp.zeros(out_ref.shape, out_ref.dtype)
    for a in range(2):
        index = index_ref[2 * a]
        x = arrived_ref[index].astype(F32)
        heads = []
        for k in range(2):
            d = down_ref[a, k].astype(F32)
            acc = None
            for i in range(rows):
                term = d[:, i * lanes : (i + 1) * lanes] * x[i : i + 1]
                acc = term if acc is None else acc + term
            reduced = jnp.sum(acc, axis=1, keepdims=True).astype(BF16).astype(F32)
            lifted = jnp.sum(reduced * up_ref[a, k].astype(F32), axis=0, keepdims=True)
            heads += [lifted[:, h * HD : (h + 1) * HD] for h in range(KVH)]
        lifted = (jnp.concatenate(heads, axis=0) * ADAPTER_SCALE).astype(out_ref.dtype)

        @pl.when(index_ref[2 * a + 1] == 1)
        def _():
            out_ref[index] = lifted


def attention_kernel(
    length_ref, mark_ref, before_ref, spread_ref, after_ref, key_ref, value_ref, out_ref
):
    span = key_ref.shape[1]
    t = lax.axis_index("tensor")
    length = length_ref[0]
    k = key_ref[0]
    v = value_ref[0]
    scores = []
    for g in range(KVH):
        place = jnp.bitwise_and(g - lax.shift_right_logical(t, 1) + 4, 7)
        row = lax.shift_right_logical(place * 11, 5)
        part = place - 3 * row
        q = jnp.where(
            part == 0,
            before_ref[row],
            jnp.where(part == 1, spread_ref[row], after_ref[row]),
        ).astype(BF16)
        scores.append(
            lax.dot_general(
                q,
                k[:, g * HD : (g + 1) * HD],
                (((1,), (1,)), ((), ())),
                preferred_element_type=F32,
            )
        )
    s = jnp.concatenate(scores, axis=0) * (1.0 / math.sqrt(HD))
    live = (t * span + lax.broadcasted_iota(jnp.int32, s.shape, 1)) < length
    s = jnp.where(live, s, MASKED)
    top = jnp.max(s, axis=1, keepdims=True)
    w = jnp.where(live, jnp.exp(s - top), 0.0)
    total = jnp.sum(w, axis=1, keepdims=True)
    wb = w.astype(BF16)
    lane = lax.broadcasted_iota(jnp.int32, (QH, HD), 1)
    head = jnp.bitwise_and(lax.broadcasted_iota(jnp.int32, (QH, HD), 0), 3)
    stats = jnp.where(lane == head, top, 0.0) + jnp.where(lane == head + 4, total, 0.0)
    zero = jnp.zeros((3, HD), F32)
    for g in range(KVH):
        acc = jnp.dot(
            wb[g * GROUP : (g + 1) * GROUP],
            v[:, g * HD : (g + 1) * HD],
            preferred_element_type=F32,
        )
        for half in range(2):
            rows = slice(4 * half, 4 * half + 4)
            stat = jnp.sum(stats[g * GROUP : (g + 1) * GROUP][rows], axis=0, keepdims=True)
            out_ref[2 * g + half] = jnp.concatenate([acc[rows], zero, stat], axis=0)


def pack_kernel(index_ref, arrived_ref, base_ref, partial_ref, out_ref):
    t = lax.axis_index("tensor")
    owner = index_ref[4]
    row = lax.broadcasted_iota(jnp.int32, (2 * KVH, HD), 0)
    p = arrived_ref[owner].astype(F32) + jnp.where(row == t, base_ref[...], 0.0)
    out_ref[...] = partial_ref[...]
    for d in range(out_ref.shape[0]):
        g = d // 2
        out_ref[d, 4:7, :] = jnp.concatenate(
            [p[d : d + 1], p[g : g + 1], p[KVH + g : KVH + g + 1]], axis=0
        )


def merge_kernel(rot_ref, query_ref, arrived_ref, fresh_ref, attended_ref):
    r = arrived_ref[...]
    n = r.shape[0]
    sums = jnp.sum(r, axis=0)
    own, key, value = sums[4:5], sums[5:6], sums[6:7]
    half = HD // 2
    own = own * rot_ref[2:3] + pltpu.roll(own, half, 1) * rot_ref[3:4]
    key = key * rot_ref[0:1] + pltpu.roll(key, half, 1) * rot_ref[1:2]
    fresh_ref[...] = own.astype(BF16)
    key = key.astype(BF16).astype(F32)
    value = value.astype(BF16).astype(F32)
    q = query_ref[...].astype(F32)
    q = jnp.concatenate([q[:, j * HD : (j + 1) * HD] for j in range(4)], axis=0)
    new_score = jnp.sum(q * key, axis=1, keepdims=True) * (1.0 / math.sqrt(HD))
    shape = (n, 8, HD)
    picked = lax.broadcasted_iota(jnp.int32, shape, 1) == lax.broadcasted_iota(
        jnp.int32, shape, 2
    )
    stats = jnp.sum(
        jnp.where(picked, jnp.broadcast_to(r[:, 7:8, :], shape), 0.0), axis=2, keepdims=True
    )
    tops, totals = stats[:, :4], stats[:, 4:]
    highest = jnp.maximum(jnp.max(tops, axis=0), new_score)
    factors = jnp.exp(tops - highest[None])
    weight = jnp.exp(new_score - highest)
    denom = jnp.sum(factors * totals, axis=0) + weight
    summed = jnp.sum(factors * r[:, :4, :], axis=0) + weight.astype(BF16).astype(F32) * value
    result = (summed / denom).astype(BF16).astype(F32)
    for j in range(4):
        attended_ref[:, j * HD : (j + 1) * HD] = result[j : j + 1].astype(BF16)


def local(
    hidden,
    key_value_weight,
    adapter_down_maps,
    adapter_up_maps,
    session_slot,
    lengths,
    queries,
    cached_key_rows,
    cached_value_rows,
):
    n_sess = lax.axis_size("sess")
    n_tensor = lax.axis_size("tensor")
    t = lax.axis_index("tensor")
    slots, two, ranks, width = adapter_down_maps.shape
    shape = jax.ShapeDtypeStruct

    parts, own_queries, index, down, up = pl.pallas_call(
        spread_kernel,
        out_shape=(
            pltpu.HBM((n_sess, 16, width // 16), BF16),
            shape((8, HD), F32),
            pltpu.SMEM((8,), jnp.int32),
            shape(adapter_down_maps.shape, BF16),
            shape(adapter_up_maps.shape, BF16),
        ),
        in_specs=[HBM] * 5,
        out_specs=(HBM, VMEM, SMEM, VMEM, VMEM),
        scratch_shapes=[
            pltpu.SMEM((n_sess,), jnp.int32),
            pltpu.VMEM(hidden.shape, BF16),
            pltpu.VMEM(queries.shape, BF16),
            pltpu.VMEM((n_sess, 16, width // 16), BF16),
            pltpu.SemaphoreType.DMA((5,)),
            pltpu.SemaphoreType.DMA((4,)),
        ],
        cost_estimate=pl.CostEstimate(flops=10**5, bytes_accessed=10**5, transcendentals=0),
        compiler_params=pltpu.CompilerParams(vmem_limit_bytes=24 * 1024 * 1024),
    )(
        *(
            pltpu.with_memory_space_constraint(x, pltpu.HBM)
            for x in (session_slot, hidden, queries, adapter_down_maps, adapter_up_maps)
        )
    )
    parts = lax.all_to_all(parts, "sess", 0, 0, tiled=True)

    def come(x, distance):
        return lax.ppermute(
            x, "tensor", [(i, (i - 2 * distance) % n_tensor) for i in range(n_tensor)]
        )

    pair = own_queries + lax.ppermute(
        own_queries, "tensor", [(i, i ^ 1) for i in range(n_tensor)]
    )
    pair = pair[None]
    spread = jnp.concatenate([come(pair, -3), pair, come(pair, 3)])
    before, after = come(spread, -1), come(spread, 1)

    terms, mark = call(
        adapter_kernel,
        (pltpu.HBM((n_sess, 2 * KVH, HD), F32), pltpu.SMEM((8,), jnp.int32)),
        [SMEM, VMEM, VMEM, VMEM, ANY],
        [index, parts, down, up, spread],
        10**6,
    )
    terms = lax.all_to_all(terms, "sess", 0, 0, tiled=True)

    partial = call(
        attention_kernel,
        shape((n_tensor, 8, HD), F32),
        [SMEM, SMEM, VMEM, VMEM, VMEM, VMEM, VMEM],
        [lengths, mark, before, spread, after, cached_key_rows, cached_value_rows],
        10**7,
    )
    base = jnp.dot(hidden, key_value_weight, preferred_element_type=F32)
    packed = call(
        pack_kernel,
        pltpu.HBM((n_tensor, 8, HD), F32),
        [SMEM, VMEM, VMEM, VMEM],
        [index, terms, base, partial],
        10**5,
    )
    packed = lax.all_to_all(packed, "tensor", 0, 0, tiled=True)

    half = HD // 2
    inverse = jnp.exp(-(2.0 * jnp.arange(half, dtype=F32) / HD) * math.log(ROPE_BASE))
    angles = lengths[0].astype(F32) * inverse
    cosine, sine = jnp.cos(angles), jnp.sin(angles)
    cosine = jnp.concatenate([cosine, cosine])
    sine = jnp.concatenate([-sine, sine])
    keyed = t < KVH
    rot = jnp.stack(
        [cosine, sine, jnp.where(keyed, cosine, 1.0), jnp.where(keyed, sine, 0.0)]
    )
    return call(
        merge_kernel,
        (shape((1, HD), BF16), shape((1, 4 * HD), BF16)),
        [VMEM, VMEM, VMEM],
        [rot, queries, packed],
        10**5,
    )


def solution(mesh):
    return jax.shard_map(
        local,
        mesh=mesh,
        in_specs=(
            P("sess", None),
            P(None, "tensor"),
            P("sess", None, "tensor", None),
            P("sess", None, "tensor", None),
            P(),
            P("sess"),
            P("sess", "tensor"),
            P("sess", "tensor", None),
            P("sess", "tensor", None),
        ),
        out_specs=(P("sess", "tensor"), P("sess", "tensor")),
        check_vma=False,
    )
```

```python
import math

import jax
import jax.numpy as jnp
from jax import lax
from jax.experimental import pallas as pl
from jax.experimental.pallas import tpu as pltpu
from jax.sharding import PartitionSpec as P

QH = 64
KVH = 8
HD = 128
GROUP = QH // KVH
ADAPTER_SCALE = 0.5
ROPE_BASE = 500000.0
MASKED = -1e30
F32 = jnp.float32
BF16 = jnp.bfloat16

VMEM = pl.BlockSpec(memory_space=pltpu.VMEM)
SMEM = pl.BlockSpec(memory_space=pltpu.SMEM)
HBM = pl.BlockSpec(memory_space=pltpu.HBM)


def call(body, out_shape, specs, args, cost):
    return pl.pallas_call(
        body,
        out_shape=out_shape,
        in_specs=specs,
        out_specs=jax.tree.map(
            lambda x: SMEM if getattr(x, "memory_space", None) == pltpu.SMEM else VMEM, out_shape
        ),
        cost_estimate=pl.CostEstimate(flops=cost, bytes_accessed=cost, transcendentals=0),
        compiler_params=pltpu.CompilerParams(vmem_limit_bytes=10 * 1024 * 1024),
    )(*args)


def holder(slot_ref, slot, n_sess):
    index = jnp.int32(0)
    found = jnp.int32(0)
    for s in range(n_sess):
        hit = slot_ref[s] == slot
        index = jnp.where(hit, jnp.int32(s), index)
        found = jnp.where(hit, jnp.int32(1), found)
    return index, found


def spread_kernel(
    slot_hbm,
    hidden_hbm,
    query_hbm,
    down_hbm,
    up_hbm,
    out_hbm,
    query_out,
    index_ref,
    shared_ref,
    own_ref,
    hidden,
    slot,
    query,
    chunks,
    sem,
    out_sem,
):
    copies = [
        pltpu.make_async_copy(hidden_hbm, hidden, sem.at[0]),
        pltpu.make_async_copy(query_hbm, query, sem.at[1]),
        pltpu.make_async_copy(slot_hbm, slot, sem.at[2]),
    ]
    n_sess, rows, lanes = out_hbm.shape
    o = lax.axis_index("sess")
    t = lax.axis_index("tensor")
    half = rows * lanes
    start = pl.multiple_of(jnp.bitwise_and(t, 1) * half, half)
    other = pl.multiple_of(half - start, half)
    up_width = up_hbm.shape[3]
    copies.append(
        pltpu.make_async_copy(
            down_hbm.at[:, :, :, pl.ds(other, half)],
            shared_ref.at[:, :, :, pl.ds(0, half)],
            sem.at[3],
        )
    )
    copies.append(
        pltpu.make_async_copy(
            up_hbm, shared_ref.at[:, :, :, pl.ds(half, up_width)], sem.at[4]
        )
    )
    copies.append(
        pltpu.make_async_copy(
            down_hbm.at[:, :, :, pl.ds(start, half)],
            own_ref.at[:, :, :, pl.ds(0, half)],
            sem.at[5],
        )
    )
    copies.append(
        pltpu.make_async_copy(up_hbm, own_ref.at[:, :, :, pl.ds(half, up_width)], sem.at[6])
    )
    for copy in copies:
        copy.start()
    copies[0].wait()
    x = hidden[:, pl.ds(start, half)].astype(F32)
    x = jnp.concatenate([x[:, j * lanes : (j + 1) * lanes] for j in range(rows)], axis=0)
    x = x.astype(BF16)
    sends = []
    step = n_sess // 4
    for s in range(4):
        places = pl.ds(s * step, step)
        chunks[places] = jnp.broadcast_to(x[None], (step, rows, lanes))
        sends.append(pltpu.make_async_copy(chunks.at[places], out_hbm.at[places], out_sem.at[s]))
        sends[-1].start()
    copies[1].wait()
    q = query[...].astype(F32)
    q = jnp.concatenate([q[:, j * HD : (j + 1) * HD] for j in range(4)], axis=0)
    even = jnp.bitwise_and(t, 1) == 0
    zero = jnp.zeros_like(q)
    upper, lower = jnp.where(even, q, zero), jnp.where(even, zero, q)
    query_out[...] = jnp.concatenate([upper, lower], axis=0)
    for a in range(2):
        shared_ref[a, 0, :, half + up_width :] = upper.astype(BF16)
        shared_ref[a, 1, :, half + up_width :] = lower.astype(BF16)
    copies[2].wait()
    for a in range(2):
        index, found = holder(slot, 2 * o + a, n_sess)
        index_ref[2 * a] = index
        index_ref[2 * a + 1] = found
    index_ref[4] = lax.shift_right_logical(slot[o], 1)
    for copy in copies[3:]:
        copy.wait()
    for send in sends:
        send.wait()


def reduce_kernel(index_ref, arrived_ref, own_ref, shared_ref, out_ref):
    rows, lanes = arrived_ref.shape[1:]
    half = rows * lanes
    for a in range(2):
        x = arrived_ref[index_ref[2 * a]].astype(F32)
        for k in range(2):
            for r, maps in enumerate((own_ref, shared_ref)):
                d = maps[a, k, :, :half].astype(F32)
                acc = None
                for i in range(rows):
                    term = d[:, i * lanes : (i + 1) * lanes] * x[i : i + 1]
                    acc = term if acc is None else acc + term
                value = jnp.sum(acc, axis=1, keepdims=True)
                out_ref[(a * 2 + k) * 2 + r] = jnp.broadcast_to(value, out_ref.shape[1:])


def lift_kernel(index_ref, mine_ref, other_ref, own_ref, shared_ref, out_ref, mark_ref):
    half = own_ref.shape[3] - KVH * HD
    k = jnp.bitwise_and(lax.axis_index("tensor"), 1)
    mark_ref[0] = jnp.int32(0)
    out_ref[...] = jnp.zeros(out_ref.shape, out_ref.dtype)
    for a in range(2):
        lifted = None
        for r, maps in enumerate((own_ref, shared_ref)):
            at = (a * 2 + k) * 2
            reduced = (mine_ref[at + r] + other_ref[at + 1 - r])[:, :1].astype(BF16).astype(F32)
            u = maps[a, k][:, half : half + KVH * HD].astype(F32)
            part = jnp.sum(reduced * u, axis=0, keepdims=True)
            lifted = part if lifted is None else lifted + part
        heads = [lifted[:, h * HD : (h + 1) * HD] for h in range(KVH)]
        lifted = jnp.concatenate(heads, axis=0) * ADAPTER_SCALE
        index = index_ref[2 * a]

        @pl.when(index_ref[2 * a + 1] == 1)
        def _():
            out_ref[index] = lifted


def attention_kernel(
    length_ref, mark_ref, near_ref, far_ref, key_ref, value_ref, out_ref
):
    span = key_ref.shape[1]
    t = lax.axis_index("tensor")
    length = length_ref[0]
    k = key_ref[0]
    v = value_ref[0]
    scores = []
    for g in range(KVH):
        away = jnp.bitwise_xor(lax.shift_right_logical(t, 1), g)
        row = lax.shift_right_logical(away, 1)
        q = jnp.where(jnp.bitwise_and(away, 1) == 0, near_ref[row], far_ref[row]).astype(BF16)
        scores.append(
            lax.dot_general(
                q,
                k[:, g * HD : (g + 1) * HD],
                (((1,), (1,)), ((), ())),
                preferred_element_type=F32,
            )
        )
    s = jnp.concatenate(scores, axis=0) * (1.0 / math.sqrt(HD))
    live = (t * span + lax.broadcasted_iota(jnp.int32, s.shape, 1)) < length
    s = jnp.where(live, s, MASKED)
    top = jnp.max(s, axis=1, keepdims=True)
    w = jnp.where(live, jnp.exp(s - top), 0.0)
    total = jnp.sum(w, axis=1, keepdims=True)
    wb = w.astype(BF16)
    lane = lax.broadcasted_iota(jnp.int32, (QH, HD), 1)
    head = jnp.bitwise_and(lax.broadcasted_iota(jnp.int32, (QH, HD), 0), 3)
    stats = jnp.where(lane == head, top, 0.0) + jnp.where(lane == head + 4, total, 0.0)
    zero = jnp.zeros((3, HD), F32)
    for g in range(KVH):
        acc = jnp.dot(
            wb[g * GROUP : (g + 1) * GROUP],
            v[:, g * HD : (g + 1) * HD],
            preferred_element_type=F32,
        )
        for half in range(2):
            rows = slice(4 * half, 4 * half + 4)
            stat = jnp.sum(stats[g * GROUP : (g + 1) * GROUP][rows], axis=0, keepdims=True)
            out_ref[2 * g + half] = jnp.concatenate([acc[rows], zero, stat], axis=0)


def base_kernel(mark_ref, hidden_ref, weight_ref, out_ref):
    out_ref[...] = jnp.dot(hidden_ref[...], weight_ref[...], preferred_element_type=F32)


def pack_kernel(index_ref, arrived_ref, base_ref, partial_ref, out_ref):
    t = lax.axis_index("tensor")
    owner = index_ref[4]
    row = lax.broadcasted_iota(jnp.int32, (2 * KVH, HD), 0)
    r = arrived_ref[owner]
    keys = jnp.bitwise_and(t, 1) == 0
    zero = jnp.zeros_like(r)
    p = jnp.concatenate([jnp.where(keys, r, zero), jnp.where(keys, zero, r)], axis=0)
    p = p + jnp.where(row == t, base_ref[...], 0.0)
    out_ref[...] = partial_ref[...]
    for d in range(out_ref.shape[0]):
        g = d // 2
        out_ref[d, 4:7, :] = jnp.concatenate(
            [p[d : d + 1], p[g : g + 1], p[KVH + g : KVH + g + 1]], axis=0
        )


def merge_kernel(rot_ref, query_ref, arrived_ref, fresh_ref, attended_ref):
    r = arrived_ref[...]
    n = r.shape[0]
    sums = jnp.sum(r, axis=0)
    own, key, value = sums[4:5], sums[5:6], sums[6:7]
    half = HD // 2
    own = own * rot_ref[2:3] + pltpu.roll(own, half, 1) * rot_ref[3:4]
    key = key * rot_ref[0:1] + pltpu.roll(key, half, 1) * rot_ref[1:2]
    fresh_ref[...] = own.astype(BF16)
    key = key.astype(BF16).astype(F32)
    value = value.astype(BF16).astype(F32)
    q = query_ref[...].astype(F32)
    q = jnp.concatenate([q[:, j * HD : (j + 1) * HD] for j in range(4)], axis=0)
    new_score = jnp.sum(q * key, axis=1, keepdims=True) * (1.0 / math.sqrt(HD))
    shape = (n, 8, HD)
    picked = lax.broadcasted_iota(jnp.int32, shape, 1) == lax.broadcasted_iota(
        jnp.int32, shape, 2
    )
    stats = jnp.sum(
        jnp.where(picked, jnp.broadcast_to(r[:, 7:8, :], shape), 0.0), axis=2, keepdims=True
    )
    tops, totals = stats[:, :4], stats[:, 4:]
    highest = jnp.maximum(jnp.max(tops, axis=0), new_score)
    factors = jnp.exp(tops - highest[None])
    weight = jnp.exp(new_score - highest)
    denom = jnp.sum(factors * totals, axis=0) + weight
    summed = jnp.sum(factors * r[:, :4, :], axis=0) + weight.astype(BF16).astype(F32) * value
    result = (summed / denom).astype(BF16).astype(F32)
    for j in range(4):
        attended_ref[:, j * HD : (j + 1) * HD] = result[j : j + 1].astype(BF16)


def local(
    hidden,
    key_value_weight,
    adapter_down_maps,
    adapter_up_maps,
    session_slot,
    lengths,
    queries,
    cached_key_rows,
    cached_value_rows,
):
    n_sess = lax.axis_size("sess")
    n_tensor = lax.axis_size("tensor")
    t = lax.axis_index("tensor")
    slots, two, ranks, width = adapter_down_maps.shape
    shape = jax.ShapeDtypeStruct
    half = width // 2

    parts, own_queries, index, shared, own, hidden = pl.pallas_call(
        spread_kernel,
        out_shape=(
            pltpu.HBM((n_sess, 16, half // 16), BF16),
            shape((8, HD), F32),
            pltpu.SMEM((8,), jnp.int32),
            shape((slots, two, ranks, half + KVH * HD + HD), BF16),
            shape((slots, two, ranks, half + KVH * HD), BF16),
            shape(hidden.shape, BF16),
        ),
        in_specs=[HBM] * 5,
        out_specs=(HBM, VMEM, SMEM, VMEM, VMEM, VMEM),
        scratch_shapes=[
            pltpu.SMEM((n_sess,), jnp.int32),
            pltpu.VMEM(queries.shape, BF16),
            pltpu.VMEM((n_sess, 16, half // 16), BF16),
            pltpu.SemaphoreType.DMA((7,)),
            pltpu.SemaphoreType.DMA((4,)),
        ],
        cost_estimate=pl.CostEstimate(flops=10**5, bytes_accessed=10**5, transcendentals=0),
        compiler_params=pltpu.CompilerParams(vmem_limit_bytes=10 * 1024 * 1024),
    )(
        *(
            pltpu.with_memory_space_constraint(x, pltpu.HBM)
            for x in (
                session_slot,
                hidden,
                queries,
                adapter_down_maps,
                adapter_up_maps,
            )
        )
    )
    parts = lax.all_to_all(parts, "sess", 0, 0, tiled=True)

    def swap(x, distance):
        return lax.ppermute(
            x, "tensor", [(i, i ^ (2 * distance)) for i in range(n_tensor)]
        )

    other_core = [(i, i ^ 1) for i in range(n_tensor)]
    shared = lax.ppermute(shared, "tensor", other_core)
    pair = own_queries + shared[0, :, :, half + KVH * HD :].reshape(8, HD).astype(F32)
    pair = pair[None]
    two_groups = jnp.concatenate([pair, swap(pair, 2)])
    near = jnp.concatenate([two_groups, swap(two_groups, 4)])
    far = swap(near, 1)

    mine = call(
        reduce_kernel,
        shape((slots * two * 2, ranks, HD), F32),
        [SMEM, VMEM, VMEM, VMEM],
        [index, parts, own, shared],
        10**6,
    )
    other = lax.ppermute(mine, "tensor", other_core)
    terms, mark = call(
        lift_kernel,
        (pltpu.HBM((n_sess, KVH, HD), F32), pltpu.SMEM((8,), jnp.int32)),
        [SMEM, VMEM, VMEM, VMEM, VMEM],
        [index, mine, other, own, shared],
        10**6,
    )
    terms = lax.all_to_all(terms, "sess", 0, 0, tiled=True)

    partial = call(
        attention_kernel,
        shape((n_tensor, 8, HD), F32),
        [SMEM, SMEM, VMEM, VMEM, VMEM, VMEM],
        [lengths, mark, near, far, cached_key_rows, cached_value_rows],
        10**7,
    )
    base = call(
        base_kernel,
        shape((1, HD), F32),
        [SMEM, VMEM, VMEM],
        [mark, hidden, pltpu.with_memory_space_constraint(key_value_weight, pltpu.HBM)],
        10**4,
    )
    packed = call(
        pack_kernel,
        shape((n_tensor, 8, HD), F32),
        [SMEM, VMEM, VMEM, VMEM],
        [index, terms, base, partial],
        10**5,
    )
    packed = lax.all_to_all(packed, "tensor", 0, 0, tiled=True)

    inverse = jnp.exp(-(2.0 * jnp.arange(HD // 2, dtype=F32) / HD) * math.log(ROPE_BASE))
    angles = lengths[0].astype(F32) * inverse
    cosine, sine = jnp.cos(angles), jnp.sin(angles)
    cosine = jnp.concatenate([cosine, cosine])
    sine = jnp.concatenate([-sine, sine])
    keyed = t < KVH
    rot = jnp.stack(
        [cosine, sine, jnp.where(keyed, cosine, 1.0), jnp.where(keyed, sine, 0.0)]
    )
    return call(
        merge_kernel,
        (shape((1, HD), BF16), shape((1, 4 * HD), BF16)),
        [VMEM, VMEM, VMEM],
        [rot, queries, packed],
        10**5,
    )


def solution(mesh):
    return jax.shard_map(
        local,
        mesh=mesh,
        in_specs=(
            P("sess", None),
            P(None, "tensor"),
            P("sess", None, "tensor", None),
            P("sess", None, "tensor", None),
            P(),
            P("sess"),
            P("sess", "tensor"),
            P("sess", "tensor", None),
            P("sess", "tensor", None),
        ),
        out_specs=(P("sess", "tensor"), P("sess", "tensor")),
        check_vma=False,
    )
```

```python
import math

import jax
import jax.numpy as jnp
from jax import lax
from jax.experimental import pallas as pl
from jax.experimental.pallas import tpu as pltpu
from jax.sharding import PartitionSpec as P

QH = 64
KVH = 8
HD = 128
GROUP = QH // KVH
ADAPTER_SCALE = 0.5
ROPE_BASE = 500000.0
MASKED = -1e30
F32 = jnp.float32
BF16 = jnp.bfloat16

VMEM = pl.BlockSpec(memory_space=pltpu.VMEM)
SMEM = pl.BlockSpec(memory_space=pltpu.SMEM)
HBM = pl.BlockSpec(memory_space=pltpu.HBM)
ANY = pl.BlockSpec(memory_space=pl.ANY)


def call(body, out_shape, specs, args, cost):
    return pl.pallas_call(
        body,
        out_shape=out_shape,
        in_specs=specs,
        out_specs=jax.tree.map(
            lambda x: SMEM if getattr(x, "memory_space", None) == pltpu.SMEM else VMEM, out_shape
        ),
        cost_estimate=pl.CostEstimate(flops=cost, bytes_accessed=cost, transcendentals=0),
        compiler_params=pltpu.CompilerParams(vmem_limit_bytes=10 * 1024 * 1024),
    )(*args)


def holder(slot_ref, slot, n_sess):
    index = jnp.int32(0)
    found = jnp.int32(0)
    for s in range(n_sess):
        hit = slot_ref[s] == slot
        index = jnp.where(hit, jnp.int32(s), index)
        found = jnp.where(hit, jnp.int32(1), found)
    return index, found


def spread_kernel(
    slot_hbm,
    hidden_hbm,
    query_hbm,
    down_hbm,
    up_hbm,
    out_hbm,
    query_out,
    index_ref,
    shared_ref,
    own_ref,
    hidden,
    slot,
    query,
    chunks,
    sem,
    out_sem,
):
    copies = [
        pltpu.make_async_copy(hidden_hbm, hidden, sem.at[0]),
        pltpu.make_async_copy(query_hbm, query, sem.at[1]),
        pltpu.make_async_copy(slot_hbm, slot, sem.at[2]),
    ]
    n_sess, rows, lanes = out_hbm.shape
    o = lax.axis_index("sess")
    t = lax.axis_index("tensor")
    half = rows * lanes
    start = pl.multiple_of(jnp.bitwise_and(t, 1) * half, half)
    other = pl.multiple_of(half - start, half)
    up_width = up_hbm.shape[3]
    copies.append(
        pltpu.make_async_copy(
            down_hbm.at[:, :, :, pl.ds(other, half)],
            shared_ref.at[:, :, :, pl.ds(0, half)],
            sem.at[3],
        )
    )
    copies.append(
        pltpu.make_async_copy(
            up_hbm, shared_ref.at[:, :, :, pl.ds(half, up_width)], sem.at[4]
        )
    )
    copies.append(
        pltpu.make_async_copy(
            down_hbm.at[:, :, :, pl.ds(start, half)],
            own_ref.at[:, :, :, pl.ds(0, half)],
            sem.at[5],
        )
    )
    copies.append(
        pltpu.make_async_copy(up_hbm, own_ref.at[:, :, :, pl.ds(half, up_width)], sem.at[6])
    )
    for copy in copies:
        copy.start()
    copies[0].wait()
    x = hidden[:, pl.ds(start, half)].astype(F32)
    x = jnp.concatenate([x[:, j * lanes : (j + 1) * lanes] for j in range(rows)], axis=0)
    x = x.astype(BF16)
    sends = []
    step = n_sess // 4
    for s in range(4):
        places = pl.ds(s * step, step)
        chunks[places] = jnp.broadcast_to(x[None], (step, rows, lanes))
        sends.append(pltpu.make_async_copy(chunks.at[places], out_hbm.at[places], out_sem.at[s]))
        sends[-1].start()
    copies[1].wait()
    q = query[...].astype(F32)
    q = jnp.concatenate([q[:, j * HD : (j + 1) * HD] for j in range(4)], axis=0)
    even = jnp.bitwise_and(t, 1) == 0
    zero = jnp.zeros_like(q)
    upper, lower = jnp.where(even, q, zero), jnp.where(even, zero, q)
    query_out[...] = jnp.concatenate([upper, lower], axis=0)
    for a in range(2):
        shared_ref[a, 0, :, half + up_width :] = upper.astype(BF16)
        shared_ref[a, 1, :, half + up_width :] = lower.astype(BF16)
    copies[2].wait()
    for a in range(2):
        index, found = holder(slot, 2 * o + a, n_sess)
        index_ref[2 * a] = index
        index_ref[2 * a + 1] = found
    index_ref[4] = lax.shift_right_logical(slot[o], 1)
    for copy in copies[3:]:
        copy.wait()
    for send in sends:
        send.wait()


def reduce_kernel(index_ref, arrived_ref, own_ref, shared_ref, groups_ref, out_ref):
    rows, lanes = arrived_ref.shape[1:]
    half = rows * lanes
    for a in range(2):
        x = arrived_ref[index_ref[2 * a]].astype(F32)
        for k in range(2):
            for r, maps in enumerate((own_ref, shared_ref)):
                d = maps[a, k, :, :half].astype(F32)
                acc = None
                for i in range(rows):
                    term = d[:, i * lanes : (i + 1) * lanes] * x[i : i + 1]
                    acc = term if acc is None else acc + term
                value = jnp.sum(acc, axis=1, keepdims=True)
                out_ref[(a * 2 + k) * 2 + r] = jnp.broadcast_to(value, out_ref.shape[1:])


def lift_kernel(index_ref, mine_ref, other_ref, own_ref, shared_ref, out_ref, mark_ref):
    half = own_ref.shape[3] - KVH * HD
    k = jnp.bitwise_and(lax.axis_index("tensor"), 1)
    mark_ref[0] = jnp.int32(0)
    out_ref[...] = jnp.zeros(out_ref.shape, out_ref.dtype)
    for a in range(2):
        lifted = None
        for r, maps in enumerate((own_ref, shared_ref)):
            at = (a * 2 + k) * 2
            reduced = (mine_ref[at + r] + other_ref[at + 1 - r])[:, :1].astype(BF16).astype(F32)
            u = maps[a, k][:, half : half + KVH * HD].astype(F32)
            part = jnp.sum(reduced * u, axis=0, keepdims=True)
            lifted = part if lifted is None else lifted + part
        heads = [lifted[:, h * HD : (h + 1) * HD] for h in range(KVH)]
        lifted = jnp.concatenate(heads, axis=0) * ADAPTER_SCALE
        index = index_ref[2 * a]

        @pl.when(index_ref[2 * a + 1] == 1)
        def _():
            out_ref[index] = lifted


def attention_kernel(
    length_ref, mark_ref, near_ref, far_ref, key_ref, value_ref, out_ref
):
    span = key_ref.shape[1]
    t = lax.axis_index("tensor")
    length = length_ref[0]
    k = key_ref[0]
    v = value_ref[0]
    scores = []
    for g in range(KVH):
        away = jnp.bitwise_xor(lax.shift_right_logical(t, 1), g)
        row = lax.shift_right_logical(away, 1)
        q = jnp.where(jnp.bitwise_and(away, 1) == 0, near_ref[row], far_ref[row]).astype(BF16)
        scores.append(
            lax.dot_general(
                q,
                k[:, g * HD : (g + 1) * HD],
                (((1,), (1,)), ((), ())),
                preferred_element_type=F32,
            )
        )
    s = jnp.concatenate(scores, axis=0) * (1.0 / math.sqrt(HD))
    live = (t * span + lax.broadcasted_iota(jnp.int32, s.shape, 1)) < length
    s = jnp.where(live, s, MASKED)
    top = jnp.max(s, axis=1, keepdims=True)
    w = jnp.where(live, jnp.exp(s - top), 0.0)
    total = jnp.sum(w, axis=1, keepdims=True)
    wb = w.astype(BF16)
    lane = lax.broadcasted_iota(jnp.int32, (QH, HD), 1)
    head = jnp.bitwise_and(lax.broadcasted_iota(jnp.int32, (QH, HD), 0), 3)
    stats = jnp.where(lane == head, top, 0.0) + jnp.where(lane == head + 4, total, 0.0)
    zero = jnp.zeros((3, HD), F32)
    for g in range(KVH):
        acc = jnp.dot(
            wb[g * GROUP : (g + 1) * GROUP],
            v[:, g * HD : (g + 1) * HD],
            preferred_element_type=F32,
        )
        for half in range(2):
            rows = slice(4 * half, 4 * half + 4)
            stat = jnp.sum(stats[g * GROUP : (g + 1) * GROUP][rows], axis=0, keepdims=True)
            out_ref[2 * g + half] = jnp.concatenate([acc[rows], zero, stat], axis=0)


def base_kernel(mark_ref, hidden_ref, weight_ref, out_ref):
    out_ref[...] = jnp.dot(hidden_ref[...], weight_ref[...], preferred_element_type=F32)


def pack_kernel(index_ref, arrived_ref, base_ref, partial_ref, out_ref):
    t = lax.axis_index("tensor")
    owner = index_ref[4]
    row = lax.broadcasted_iota(jnp.int32, (2 * KVH, HD), 0)
    r = arrived_ref[owner]
    keys = jnp.bitwise_and(t, 1) == 0
    zero = jnp.zeros_like(r)
    p = jnp.concatenate([jnp.where(keys, r, zero), jnp.where(keys, zero, r)], axis=0)
    p = p + jnp.where(row == t, base_ref[...], 0.0)
    out_ref[...] = partial_ref[...]
    for d in range(out_ref.shape[0]):
        g = d // 2
        out_ref[d, 4:7, :] = jnp.concatenate(
            [p[d : d + 1], p[g : g + 1], p[KVH + g : KVH + g + 1]], axis=0
        )


def merge_kernel(rot_ref, query_ref, arrived_ref, fresh_ref, attended_ref):
    r = arrived_ref[...]
    n = r.shape[0]
    sums = jnp.sum(r, axis=0)
    own, key, value = sums[4:5], sums[5:6], sums[6:7]
    half = HD // 2
    own = own * rot_ref[2:3] + pltpu.roll(own, half, 1) * rot_ref[3:4]
    key = key * rot_ref[0:1] + pltpu.roll(key, half, 1) * rot_ref[1:2]
    fresh_ref[...] = own.astype(BF16)
    key = key.astype(BF16).astype(F32)
    value = value.astype(BF16).astype(F32)
    q = query_ref[...].astype(F32)
    q = jnp.concatenate([q[:, j * HD : (j + 1) * HD] for j in range(4)], axis=0)
    new_score = jnp.sum(q * key, axis=1, keepdims=True) * (1.0 / math.sqrt(HD))
    shape = (n, 8, HD)
    picked = lax.broadcasted_iota(jnp.int32, shape, 1) == lax.broadcasted_iota(
        jnp.int32, shape, 2
    )
    stats = jnp.sum(
        jnp.where(picked, jnp.broadcast_to(r[:, 7:8, :], shape), 0.0), axis=2, keepdims=True
    )
    tops, totals = stats[:, :4], stats[:, 4:]
    highest = jnp.maximum(jnp.max(tops, axis=0), new_score)
    factors = jnp.exp(tops - highest[None])
    weight = jnp.exp(new_score - highest)
    denom = jnp.sum(factors * totals, axis=0) + weight
    summed = jnp.sum(factors * r[:, :4, :], axis=0) + weight.astype(BF16).astype(F32) * value
    result = (summed / denom).astype(BF16).astype(F32)
    for j in range(4):
        attended_ref[:, j * HD : (j + 1) * HD] = result[j : j + 1].astype(BF16)


def local(
    hidden,
    key_value_weight,
    adapter_down_maps,
    adapter_up_maps,
    session_slot,
    lengths,
    queries,
    cached_key_rows,
    cached_value_rows,
):
    n_sess = lax.axis_size("sess")
    n_tensor = lax.axis_size("tensor")
    t = lax.axis_index("tensor")
    slots, two, ranks, width = adapter_down_maps.shape
    shape = jax.ShapeDtypeStruct
    half = width // 2

    parts, own_queries, index, shared, own, hidden = pl.pallas_call(
        spread_kernel,
        out_shape=(
            pltpu.HBM((n_sess, 16, half // 16), BF16),
            shape((8, HD), F32),
            pltpu.SMEM((8,), jnp.int32),
            shape((slots, two, ranks, half + KVH * HD + HD), BF16),
            shape((slots, two, ranks, half + KVH * HD), BF16),
            shape(hidden.shape, BF16),
        ),
        in_specs=[HBM] * 5,
        out_specs=(HBM, VMEM, SMEM, VMEM, VMEM, VMEM),
        scratch_shapes=[
            pltpu.SMEM((n_sess,), jnp.int32),
            pltpu.VMEM(queries.shape, BF16),
            pltpu.VMEM((n_sess, 16, half // 16), BF16),
            pltpu.SemaphoreType.DMA((7,)),
            pltpu.SemaphoreType.DMA((4,)),
        ],
        cost_estimate=pl.CostEstimate(flops=10**5, bytes_accessed=10**5, transcendentals=0),
        compiler_params=pltpu.CompilerParams(vmem_limit_bytes=10 * 1024 * 1024),
    )(
        *(
            pltpu.with_memory_space_constraint(x, pltpu.HBM)
            for x in (
                session_slot,
                hidden,
                queries,
                adapter_down_maps,
                adapter_up_maps,
            )
        )
    )
    parts = lax.all_to_all(parts, "sess", 0, 0, tiled=True)

    def swap(x, distance):
        return lax.ppermute(
            x, "tensor", [(i, i ^ (2 * distance)) for i in range(n_tensor)]
        )

    other_core = [(i, i ^ 1) for i in range(n_tensor)]
    shared = lax.ppermute(shared, "tensor", other_core)
    pair = own_queries + shared[0, :, :, half + KVH * HD :].reshape(8, HD).astype(F32)
    pair = pair[None]
    two_groups = jnp.concatenate([pair, swap(pair, 2)])
    near = jnp.concatenate([two_groups, swap(two_groups, 4)])
    far = swap(near, 1)

    mine = call(
        reduce_kernel,
        shape((slots * two * 2, ranks, HD), F32),
        [SMEM, VMEM, VMEM, VMEM, ANY],
        [index, parts, own, shared, two_groups],
        10**6,
    )
    other = lax.ppermute(mine, "tensor", other_core)
    terms, mark = call(
        lift_kernel,
        (pltpu.HBM((n_sess, KVH, HD), F32), pltpu.SMEM((8,), jnp.int32)),
        [SMEM, VMEM, VMEM, VMEM, VMEM],
        [index, mine, other, own, shared],
        10**6,
    )
    terms = lax.all_to_all(terms, "sess", 0, 0, tiled=True)

    partial = call(
        attention_kernel,
        shape((n_tensor, 8, HD), F32),
        [SMEM, SMEM, VMEM, VMEM, VMEM, VMEM],
        [lengths, mark, near, far, cached_key_rows, cached_value_rows],
        10**7,
    )
    base = call(
        base_kernel,
        shape((1, HD), F32),
        [SMEM, VMEM, VMEM],
        [mark, hidden, pltpu.with_memory_space_constraint(key_value_weight, pltpu.HBM)],
        10**4,
    )
    packed = call(
        pack_kernel,
        shape((n_tensor, 8, HD), F32),
        [SMEM, VMEM, VMEM, VMEM],
        [index, terms, base, partial],
        10**5,
    )
    packed = lax.all_to_all(packed, "tensor", 0, 0, tiled=True)

    inverse = jnp.exp(-(2.0 * jnp.arange(HD // 2, dtype=F32) / HD) * math.log(ROPE_BASE))
    angles = lengths[0].astype(F32) * inverse
    cosine, sine = jnp.cos(angles), jnp.sin(angles)
    cosine = jnp.concatenate([cosine, cosine])
    sine = jnp.concatenate([-sine, sine])
    keyed = t < KVH
    rot = jnp.stack(
        [cosine, sine, jnp.where(keyed, cosine, 1.0), jnp.where(keyed, sine, 0.0)]
    )
    return call(
        merge_kernel,
        (shape((1, HD), BF16), shape((1, 4 * HD), BF16)),
        [VMEM, VMEM, VMEM],
        [rot, queries, packed],
        10**5,
    )


def solution(mesh):
    return jax.shard_map(
        local,
        mesh=mesh,
        in_specs=(
            P("sess", None),
            P(None, "tensor"),
            P("sess", None, "tensor", None),
            P("sess", None, "tensor", None),
            P(),
            P("sess"),
            P("sess", "tensor"),
            P("sess", "tensor", None),
            P("sess", "tensor", None),
        ),
        out_specs=(P("sess", "tensor"), P("sess", "tensor")),
        check_vma=False,
    )
```

```python
import math

import jax
import jax.numpy as jnp
from jax import lax
from jax.experimental import pallas as pl
from jax.experimental.pallas import tpu as pltpu
from jax.sharding import PartitionSpec as P

QH = 64
KVH = 8
HD = 128
GROUP = QH // KVH
ADAPTER_SCALE = 0.5
ROPE_BASE = 500000.0
MASKED = -1e30
F32 = jnp.float32
BF16 = jnp.bfloat16

VMEM = pl.BlockSpec(memory_space=pltpu.VMEM)
SMEM = pl.BlockSpec(memory_space=pltpu.SMEM)
HBM = pl.BlockSpec(memory_space=pltpu.HBM)
ANY = pl.BlockSpec(memory_space=pl.ANY)


def call(body, out_shape, specs, args, cost):
    return pl.pallas_call(
        body,
        out_shape=out_shape,
        in_specs=specs,
        out_specs=jax.tree.map(
            lambda x: SMEM if getattr(x, "memory_space", None) == pltpu.SMEM else VMEM, out_shape
        ),
        cost_estimate=pl.CostEstimate(flops=cost, bytes_accessed=cost, transcendentals=0),
        compiler_params=pltpu.CompilerParams(vmem_limit_bytes=10 * 1024 * 1024),
    )(*args)


def holder(slot_ref, slot, n_sess):
    index = jnp.int32(0)
    found = jnp.int32(0)
    for s in range(n_sess):
        hit = slot_ref[s] == slot
        index = jnp.where(hit, jnp.int32(s), index)
        found = jnp.where(hit, jnp.int32(1), found)
    return index, found


def spread_kernel(
    slot_hbm,
    hidden_hbm,
    query_hbm,
    down_hbm,
    up_hbm,
    out_hbm,
    query_out,
    index_ref,
    shared_ref,
    own_ref,
    hidden,
    slot,
    query,
    chunks,
    sem,
    out_sem,
):
    copies = [
        pltpu.make_async_copy(hidden_hbm, hidden, sem.at[0]),
        pltpu.make_async_copy(query_hbm, query, sem.at[1]),
        pltpu.make_async_copy(slot_hbm, slot, sem.at[2]),
    ]
    n_sess, rows, lanes = out_hbm.shape
    o = lax.axis_index("sess")
    t = lax.axis_index("tensor")
    half = rows * lanes
    start = pl.multiple_of(jnp.bitwise_and(t, 1) * half, half)
    other = pl.multiple_of(half - start, half)
    up_width = up_hbm.shape[3]
    copies.append(
        pltpu.make_async_copy(
            down_hbm.at[:, :, :, pl.ds(other, half)],
            shared_ref.at[:, :, :, pl.ds(0, half)],
            sem.at[3],
        )
    )
    copies.append(
        pltpu.make_async_copy(
            up_hbm, shared_ref.at[:, :, :, pl.ds(half, up_width)], sem.at[4]
        )
    )
    copies.append(
        pltpu.make_async_copy(
            down_hbm.at[:, :, :, pl.ds(start, half)],
            own_ref.at[:, :, :, pl.ds(0, half)],
            sem.at[5],
        )
    )
    copies.append(
        pltpu.make_async_copy(up_hbm, own_ref.at[:, :, :, pl.ds(half, up_width)], sem.at[6])
    )
    for copy in copies:
        copy.start()
    copies[0].wait()
    x = hidden[:, pl.ds(start, half)].astype(F32)
    x = jnp.concatenate([x[:, j * lanes : (j + 1) * lanes] for j in range(rows)], axis=0)
    x = x.astype(BF16)
    sends = []
    step = n_sess // 4
    for s in range(4):
        places = pl.ds(s * step, step)
        chunks[places] = jnp.broadcast_to(x[None], (step, rows, lanes))
        sends.append(pltpu.make_async_copy(chunks.at[places], out_hbm.at[places], out_sem.at[s]))
        sends[-1].start()
    copies[1].wait()
    q = query[...].astype(F32)
    q = jnp.concatenate([q[:, j * HD : (j + 1) * HD] for j in range(4)], axis=0)
    even = jnp.bitwise_and(t, 1) == 0
    zero = jnp.zeros_like(q)
    upper, lower = jnp.where(even, q, zero), jnp.where(even, zero, q)
    query_out[...] = jnp.concatenate([upper, lower], axis=0)
    for a in range(2):
        shared_ref[a, 0, :, half + up_width :] = upper.astype(BF16)
        shared_ref[a, 1, :, half + up_width :] = lower.astype(BF16)
    copies[2].wait()
    for a in range(2):
        index, found = holder(slot, 2 * o + a, n_sess)
        index_ref[2 * a] = index
        index_ref[2 * a + 1] = found
    index_ref[4] = lax.shift_right_logical(slot[o], 1)
    for copy in copies[3:]:
        copy.wait()
    for send in sends:
        send.wait()


def reduce_kernel(index_ref, arrived_ref, own_ref, shared_ref, groups_ref, out_ref):
    rows, lanes = arrived_ref.shape[1:]
    half = rows * lanes
    for a in range(2):
        x = arrived_ref[index_ref[2 * a]].astype(F32)
        for k in range(2):
            for r, maps in enumerate((own_ref, shared_ref)):
                d = maps[a, k, :, :half].astype(F32)
                acc = None
                for i in range(rows):
                    term = d[:, i * lanes : (i + 1) * lanes] * x[i : i + 1]
                    acc = term if acc is None else acc + term
                value = jnp.sum(acc, axis=1, keepdims=True)
                out_ref[(a * 2 + k) * 2 + r] = jnp.broadcast_to(value, out_ref.shape[1:])


def lift_kernel(index_ref, mine_ref, other_ref, own_ref, shared_ref, out_ref, mark_ref):
    half = own_ref.shape[3] - KVH * HD
    k = jnp.bitwise_and(lax.axis_index("tensor"), 1)
    mark_ref[0] = jnp.int32(0)
    out_ref[...] = jnp.zeros(out_ref.shape, out_ref.dtype)
    for a in range(2):
        lifted = None
        for r, maps in enumerate((own_ref, shared_ref)):
            at = (a * 2 + k) * 2
            reduced = (mine_ref[at + r] + other_ref[at + 1 - r])[:, :1].astype(BF16).astype(F32)
            u = maps[a, k][:, half : half + KVH * HD].astype(F32)
            part = jnp.sum(reduced * u, axis=0, keepdims=True)
            lifted = part if lifted is None else lifted + part
        heads = [lifted[:, h * HD : (h + 1) * HD] for h in range(KVH)]
        lifted = jnp.concatenate(heads, axis=0) * ADAPTER_SCALE
        index = index_ref[2 * a]

        @pl.when(index_ref[2 * a + 1] == 1)
        def _():
            out_ref[index] = lifted


def attention_kernel(
    length_ref, mark_ref, near_ref, far_ref, key_ref, value_ref, out_ref
):
    span = key_ref.shape[1]
    t = lax.axis_index("tensor")
    length = length_ref[0]
    k = key_ref[0]
    v = value_ref[0]
    scores = []
    for g in range(KVH):
        away = jnp.bitwise_xor(lax.shift_right_logical(t, 1), g)
        row = lax.shift_right_logical(away, 2) + jnp.bitwise_and(away, 2)
        q = jnp.where(jnp.bitwise_and(away, 1) == 0, near_ref[row], far_ref[row]).astype(BF16)
        scores.append(
            lax.dot_general(
                q,
                k[:, g * HD : (g + 1) * HD],
                (((1,), (1,)), ((), ())),
                preferred_element_type=F32,
            )
        )
    s = jnp.concatenate(scores, axis=0) * (1.0 / math.sqrt(HD))
    live = (t * span + lax.broadcasted_iota(jnp.int32, s.shape, 1)) < length
    s = jnp.where(live, s, MASKED)
    top = jnp.max(s, axis=1, keepdims=True)
    w = jnp.where(live, jnp.exp(s - top), 0.0)
    total = jnp.sum(w, axis=1, keepdims=True)
    wb = w.astype(BF16)
    lane = lax.broadcasted_iota(jnp.int32, (QH, HD), 1)
    head = jnp.bitwise_and(lax.broadcasted_iota(jnp.int32, (QH, HD), 0), 3)
    stats = jnp.where(lane == head, top, 0.0) + jnp.where(lane == head + 4, total, 0.0)
    zero = jnp.zeros((3, HD), F32)
    for g in range(KVH):
        acc = jnp.dot(
            wb[g * GROUP : (g + 1) * GROUP],
            v[:, g * HD : (g + 1) * HD],
            preferred_element_type=F32,
        )
        for half in range(2):
            rows = slice(4 * half, 4 * half + 4)
            stat = jnp.sum(stats[g * GROUP : (g + 1) * GROUP][rows], axis=0, keepdims=True)
            out_ref[2 * g + half] = jnp.concatenate([acc[rows], zero, stat], axis=0)


def base_kernel(mark_ref, hidden_ref, weight_ref, out_ref):
    out_ref[...] = jnp.dot(hidden_ref[...], weight_ref[...], preferred_element_type=F32)


def pack_kernel(index_ref, arrived_ref, base_ref, partial_ref, out_ref):
    t = lax.axis_index("tensor")
    owner = index_ref[4]
    row = lax.broadcasted_iota(jnp.int32, (2 * KVH, HD), 0)
    r = arrived_ref[owner]
    keys = jnp.bitwise_and(t, 1) == 0
    zero = jnp.zeros_like(r)
    p = jnp.concatenate([jnp.where(keys, r, zero), jnp.where(keys, zero, r)], axis=0)
    p = p + jnp.where(row == t, base_ref[...], 0.0)
    out_ref[...] = partial_ref[...]
    for d in range(out_ref.shape[0]):
        g = d // 2
        out_ref[d, 4:7, :] = jnp.concatenate(
            [p[d : d + 1], p[g : g + 1], p[KVH + g : KVH + g + 1]], axis=0
        )


def merge_kernel(rot_ref, query_ref, arrived_ref, fresh_ref, attended_ref):
    r = arrived_ref[...]
    n = r.shape[0]
    sums = jnp.sum(r, axis=0)
    own, key, value = sums[4:5], sums[5:6], sums[6:7]
    half = HD // 2
    own = own * rot_ref[2:3] + pltpu.roll(own, half, 1) * rot_ref[3:4]
    key = key * rot_ref[0:1] + pltpu.roll(key, half, 1) * rot_ref[1:2]
    fresh_ref[...] = own.astype(BF16)
    key = key.astype(BF16).astype(F32)
    value = value.astype(BF16).astype(F32)
    q = query_ref[...].astype(F32)
    q = jnp.concatenate([q[:, j * HD : (j + 1) * HD] for j in range(4)], axis=0)
    new_score = jnp.sum(q * key, axis=1, keepdims=True) * (1.0 / math.sqrt(HD))
    shape = (n, 8, HD)
    picked = lax.broadcasted_iota(jnp.int32, shape, 1) == lax.broadcasted_iota(
        jnp.int32, shape, 2
    )
    stats = jnp.sum(
        jnp.where(picked, jnp.broadcast_to(r[:, 7:8, :], shape), 0.0), axis=2, keepdims=True
    )
    tops, totals = stats[:, :4], stats[:, 4:]
    highest = jnp.maximum(jnp.max(tops, axis=0), new_score)
    factors = jnp.exp(tops - highest[None])
    weight = jnp.exp(new_score - highest)
    denom = jnp.sum(factors * totals, axis=0) + weight
    summed = jnp.sum(factors * r[:, :4, :], axis=0) + weight.astype(BF16).astype(F32) * value
    result = (summed / denom).astype(BF16).astype(F32)
    for j in range(4):
        attended_ref[:, j * HD : (j + 1) * HD] = result[j : j + 1].astype(BF16)


def local(
    hidden,
    key_value_weight,
    adapter_down_maps,
    adapter_up_maps,
    session_slot,
    lengths,
    queries,
    cached_key_rows,
    cached_value_rows,
):
    n_sess = lax.axis_size("sess")
    n_tensor = lax.axis_size("tensor")
    t = lax.axis_index("tensor")
    slots, two, ranks, width = adapter_down_maps.shape
    shape = jax.ShapeDtypeStruct
    half = width // 2

    parts, own_queries, index, shared, own, hidden = pl.pallas_call(
        spread_kernel,
        out_shape=(
            pltpu.HBM((n_sess, 16, half // 16), BF16),
            shape((8, HD), F32),
            pltpu.SMEM((8,), jnp.int32),
            shape((slots, two, ranks, half + KVH * HD + HD), BF16),
            shape((slots, two, ranks, half + KVH * HD), BF16),
            shape(hidden.shape, BF16),
        ),
        in_specs=[HBM] * 5,
        out_specs=(HBM, VMEM, SMEM, VMEM, VMEM, VMEM),
        scratch_shapes=[
            pltpu.SMEM((n_sess,), jnp.int32),
            pltpu.VMEM(queries.shape, BF16),
            pltpu.VMEM((n_sess, 16, half // 16), BF16),
            pltpu.SemaphoreType.DMA((7,)),
            pltpu.SemaphoreType.DMA((4,)),
        ],
        cost_estimate=pl.CostEstimate(flops=10**5, bytes_accessed=10**5, transcendentals=0),
        compiler_params=pltpu.CompilerParams(vmem_limit_bytes=10 * 1024 * 1024),
    )(
        *(
            pltpu.with_memory_space_constraint(x, pltpu.HBM)
            for x in (
                session_slot,
                hidden,
                queries,
                adapter_down_maps,
                adapter_up_maps,
            )
        )
    )
    parts = lax.all_to_all(parts, "sess", 0, 0, tiled=True)

    def swap(x, distance):
        return lax.ppermute(
            x, "tensor", [(i, i ^ (2 * distance)) for i in range(n_tensor)]
        )

    other_core = [(i, i ^ 1) for i in range(n_tensor)]
    shared = lax.ppermute(shared, "tensor", other_core)
    pair = own_queries + shared[0, :, :, half + KVH * HD :].reshape(8, HD).astype(F32)
    pair = pair[None]
    two_groups = jnp.concatenate([pair, swap(pair, 4)])
    near = jnp.concatenate([two_groups, swap(two_groups, 2)])
    far = swap(near, 1)

    mine = call(
        reduce_kernel,
        shape((slots * two * 2, ranks, HD), F32),
        [SMEM, VMEM, VMEM, VMEM, ANY],
        [index, parts, own, shared, two_groups],
        10**6,
    )
    other = lax.ppermute(mine, "tensor", other_core)
    terms, mark = call(
        lift_kernel,
        (pltpu.HBM((n_sess, KVH, HD), F32), pltpu.SMEM((8,), jnp.int32)),
        [SMEM, VMEM, VMEM, VMEM, VMEM],
        [index, mine, other, own, shared],
        10**6,
    )
    terms = lax.all_to_all(terms, "sess", 0, 0, tiled=True)

    partial = call(
        attention_kernel,
        shape((n_tensor, 8, HD), F32),
        [SMEM, SMEM, VMEM, VMEM, VMEM, VMEM],
        [lengths, mark, near, far, cached_key_rows, cached_value_rows],
        10**7,
    )
    base = call(
        base_kernel,
        shape((1, HD), F32),
        [SMEM, VMEM, VMEM],
        [mark, hidden, pltpu.with_memory_space_constraint(key_value_weight, pltpu.HBM)],
        10**4,
    )
    packed = call(
        pack_kernel,
        shape((n_tensor, 8, HD), F32),
        [SMEM, VMEM, VMEM, VMEM],
        [index, terms, base, partial],
        10**5,
    )
    packed = lax.all_to_all(packed, "tensor", 0, 0, tiled=True)

    inverse = jnp.exp(-(2.0 * jnp.arange(HD // 2, dtype=F32) / HD) * math.log(ROPE_BASE))
    angles = lengths[0].astype(F32) * inverse
    cosine, sine = jnp.cos(angles), jnp.sin(angles)
    cosine = jnp.concatenate([cosine, cosine])
    sine = jnp.concatenate([-sine, sine])
    keyed = t < KVH
    rot = jnp.stack(
        [cosine, sine, jnp.where(keyed, cosine, 1.0), jnp.where(keyed, sine, 0.0)]
    )
    return call(
        merge_kernel,
        (shape((1, HD), BF16), shape((1, 4 * HD), BF16)),
        [VMEM, VMEM, VMEM],
        [rot, queries, packed],
        10**5,
    )


def solution(mesh):
    return jax.shard_map(
        local,
        mesh=mesh,
        in_specs=(
            P("sess", None),
            P(None, "tensor"),
            P("sess", None, "tensor", None),
            P("sess", None, "tensor", None),
            P(),
            P("sess"),
            P("sess", "tensor"),
            P("sess", "tensor", None),
            P("sess", "tensor", None),
        ),
        out_specs=(P("sess", "tensor"), P("sess", "tensor")),
        check_vma=False,
    )
```

```python
import math

import jax
import jax.numpy as jnp
from jax import lax
from jax.experimental import pallas as pl
from jax.experimental.pallas import tpu as pltpu
from jax.sharding import PartitionSpec as P

QH = 64
KVH = 8
HD = 128
GROUP = QH // KVH
ADAPTER_SCALE = 0.5
ROPE_BASE = 500000.0
MASKED = -1e30
F32 = jnp.float32
BF16 = jnp.bfloat16

VMEM = pl.BlockSpec(memory_space=pltpu.VMEM)
SMEM = pl.BlockSpec(memory_space=pltpu.SMEM)
HBM = pl.BlockSpec(memory_space=pltpu.HBM)
ANY = pl.BlockSpec(memory_space=pl.ANY)


def call(body, out_shape, specs, args, cost):
    return pl.pallas_call(
        body,
        out_shape=out_shape,
        in_specs=specs,
        out_specs=jax.tree.map(
            lambda x: SMEM if getattr(x, "memory_space", None) == pltpu.SMEM else VMEM, out_shape
        ),
        cost_estimate=pl.CostEstimate(flops=cost, bytes_accessed=cost, transcendentals=0),
        compiler_params=pltpu.CompilerParams(vmem_limit_bytes=10 * 1024 * 1024),
    )(*args)


def holder(slot_ref, slot, n_sess):
    index = jnp.int32(0)
    found = jnp.int32(0)
    for s in range(n_sess):
        hit = slot_ref[s] == slot
        index = jnp.where(hit, jnp.int32(s), index)
        found = jnp.where(hit, jnp.int32(1), found)
    return index, found


def spread_kernel(
    slot_hbm,
    hidden_hbm,
    query_hbm,
    down_hbm,
    up_hbm,
    out_hbm,
    query_out,
    index_ref,
    shared_ref,
    own_ref,
    hidden,
    slot,
    query,
    chunks,
    sem,
    out_sem,
):
    copies = [
        pltpu.make_async_copy(hidden_hbm, hidden, sem.at[0]),
        pltpu.make_async_copy(query_hbm, query, sem.at[1]),
        pltpu.make_async_copy(slot_hbm, slot, sem.at[2]),
    ]
    n_sess, rows, lanes = out_hbm.shape
    o = lax.axis_index("sess")
    t = lax.axis_index("tensor")
    half = rows * lanes
    start = pl.multiple_of(jnp.bitwise_and(t, 1) * half, half)
    other = pl.multiple_of(half - start, half)
    up_width = up_hbm.shape[3]
    copies.append(
        pltpu.make_async_copy(
            down_hbm.at[:, :, :, pl.ds(other, half)],
            shared_ref.at[:, :, :, pl.ds(0, half)],
            sem.at[3],
        )
    )
    copies.append(
        pltpu.make_async_copy(
            up_hbm, shared_ref.at[:, :, :, pl.ds(half, up_width)], sem.at[4]
        )
    )
    copies.append(
        pltpu.make_async_copy(
            down_hbm.at[:, :, :, pl.ds(start, half)],
            own_ref.at[:, :, :, pl.ds(0, half)],
            sem.at[5],
        )
    )
    copies.append(
        pltpu.make_async_copy(up_hbm, own_ref.at[:, :, :, pl.ds(half, up_width)], sem.at[6])
    )
    for copy in copies:
        copy.start()
    copies[0].wait()
    x = hidden[:, pl.ds(start, half)].astype(F32)
    x = jnp.concatenate([x[:, j * lanes : (j + 1) * lanes] for j in range(rows)], axis=0)
    x = x.astype(BF16)
    sends = []
    step = n_sess // 4
    for s in range(4):
        places = pl.ds(s * step, step)
        chunks[places] = jnp.broadcast_to(x[None], (step, rows, lanes))
        sends.append(pltpu.make_async_copy(chunks.at[places], out_hbm.at[places], out_sem.at[s]))
        sends[-1].start()
    copies[1].wait()
    q = query[...].astype(F32)
    q = jnp.concatenate([q[:, j * HD : (j + 1) * HD] for j in range(4)], axis=0)
    even = jnp.bitwise_and(t, 1) == 0
    zero = jnp.zeros_like(q)
    upper, lower = jnp.where(even, q, zero), jnp.where(even, zero, q)
    query_out[...] = jnp.concatenate([upper, lower], axis=0)
    for a in range(2):
        shared_ref[a, 0, :, half + up_width :] = upper.astype(BF16)
        shared_ref[a, 1, :, half + up_width :] = lower.astype(BF16)
    copies[2].wait()
    for a in range(2):
        index, found = holder(slot, 2 * o + a, n_sess)
        index_ref[2 * a] = index
        index_ref[2 * a + 1] = found
    index_ref[4] = lax.shift_right_logical(slot[o], 1)
    for copy in copies[3:]:
        copy.wait()
    for send in sends:
        send.wait()


def reduce_kernel(index_ref, arrived_ref, own_ref, shared_ref, near_ref, out_ref):
    rows, lanes = arrived_ref.shape[1:]
    half = rows * lanes
    for a in range(2):
        x = arrived_ref[index_ref[2 * a]].astype(F32)
        for k in range(2):
            for r, maps in enumerate((own_ref, shared_ref)):
                d = maps[a, k, :, :half].astype(F32)
                acc = None
                for i in range(rows):
                    term = d[:, i * lanes : (i + 1) * lanes] * x[i : i + 1]
                    acc = term if acc is None else acc + term
                value = jnp.sum(acc, axis=1, keepdims=True)
                out_ref[(a * 2 + k) * 2 + r] = jnp.broadcast_to(value, out_ref.shape[1:])


def lift_kernel(index_ref, mine_ref, other_ref, own_ref, shared_ref, out_ref, mark_ref):
    half = own_ref.shape[3] - KVH * HD
    k = jnp.bitwise_and(lax.axis_index("tensor"), 1)
    mark_ref[0] = jnp.int32(0)
    out_ref[...] = jnp.zeros(out_ref.shape, out_ref.dtype)
    for a in range(2):
        lifted = None
        for r, maps in enumerate((own_ref, shared_ref)):
            at = (a * 2 + k) * 2
            reduced = (mine_ref[at + r] + other_ref[at + 1 - r])[:, :1].astype(BF16).astype(F32)
            u = maps[a, k][:, half : half + KVH * HD].astype(F32)
            part = jnp.sum(reduced * u, axis=0, keepdims=True)
            lifted = part if lifted is None else lifted + part
        heads = [lifted[:, h * HD : (h + 1) * HD] for h in range(KVH)]
        lifted = jnp.concatenate(heads, axis=0) * ADAPTER_SCALE
        index = index_ref[2 * a]

        @pl.when(index_ref[2 * a + 1] == 1)
        def _():
            out_ref[index] = lifted


def attention_kernel(
    length_ref, mark_ref, before_ref, near_ref, after_ref, key_ref, value_ref, out_ref
):
    span = key_ref.shape[1]
    t = lax.axis_index("tensor")
    length = length_ref[0]
    k = key_ref[0]
    v = value_ref[0]
    scores = []
    for g in range(KVH):
        place = jnp.bitwise_and(g - lax.shift_right_logical(t, 1) + 4, 7)
        row = lax.shift_right_logical(place * 11, 5)
        part = place - 3 * row
        q = jnp.where(
            part == 0,
            before_ref[row],
            jnp.where(part == 1, near_ref[row], after_ref[row]),
        ).astype(BF16)
        scores.append(
            lax.dot_general(
                q,
                k[:, g * HD : (g + 1) * HD],
                (((1,), (1,)), ((), ())),
                preferred_element_type=F32,
            )
        )
    s = jnp.concatenate(scores, axis=0) * (1.0 / math.sqrt(HD))
    live = (t * span + lax.broadcasted_iota(jnp.int32, s.shape, 1)) < length
    s = jnp.where(live, s, MASKED)
    top = jnp.max(s, axis=1, keepdims=True)
    w = jnp.where(live, jnp.exp(s - top), 0.0)
    total = jnp.sum(w, axis=1, keepdims=True)
    wb = w.astype(BF16)
    lane = lax.broadcasted_iota(jnp.int32, (QH, HD), 1)
    head = jnp.bitwise_and(lax.broadcasted_iota(jnp.int32, (QH, HD), 0), 3)
    stats = jnp.where(lane == head, top, 0.0) + jnp.where(lane == head + 4, total, 0.0)
    zero = jnp.zeros((3, HD), F32)
    for g in range(KVH):
        acc = jnp.dot(
            wb[g * GROUP : (g + 1) * GROUP],
            v[:, g * HD : (g + 1) * HD],
            preferred_element_type=F32,
        )
        for half in range(2):
            rows = slice(4 * half, 4 * half + 4)
            stat = jnp.sum(stats[g * GROUP : (g + 1) * GROUP][rows], axis=0, keepdims=True)
            out_ref[2 * g + half] = jnp.concatenate([acc[rows], zero, stat], axis=0)


def base_kernel(mark_ref, hidden_ref, weight_ref, out_ref):
    out_ref[...] = jnp.dot(hidden_ref[...], weight_ref[...], preferred_element_type=F32)


def pack_kernel(index_ref, arrived_ref, base_ref, partial_ref, out_ref):
    t = lax.axis_index("tensor")
    owner = index_ref[4]
    row = lax.broadcasted_iota(jnp.int32, (2 * KVH, HD), 0)
    r = arrived_ref[owner]
    keys = jnp.bitwise_and(t, 1) == 0
    zero = jnp.zeros_like(r)
    p = jnp.concatenate([jnp.where(keys, r, zero), jnp.where(keys, zero, r)], axis=0)
    p = p + jnp.where(row == t, base_ref[...], 0.0)
    out_ref[...] = partial_ref[...]
    for d in range(out_ref.shape[0]):
        g = d // 2
        out_ref[d, 4:7, :] = jnp.concatenate(
            [p[d : d + 1], p[g : g + 1], p[KVH + g : KVH + g + 1]], axis=0
        )


def merge_kernel(rot_ref, query_ref, arrived_ref, fresh_ref, attended_ref):
    r = arrived_ref[...]
    n = r.shape[0]
    sums = jnp.sum(r, axis=0)
    own, key, value = sums[4:5], sums[5:6], sums[6:7]
    half = HD // 2
    own = own * rot_ref[2:3] + pltpu.roll(own, half, 1) * rot_ref[3:4]
    key = key * rot_ref[0:1] + pltpu.roll(key, half, 1) * rot_ref[1:2]
    fresh_ref[...] = own.astype(BF16)
    key = key.astype(BF16).astype(F32)
    value = value.astype(BF16).astype(F32)
    q = query_ref[...].astype(F32)
    q = jnp.concatenate([q[:, j * HD : (j + 1) * HD] for j in range(4)], axis=0)
    new_score = jnp.sum(q * key, axis=1, keepdims=True) * (1.0 / math.sqrt(HD))
    shape = (n, 8, HD)
    picked = lax.broadcasted_iota(jnp.int32, shape, 1) == lax.broadcasted_iota(
        jnp.int32, shape, 2
    )
    stats = jnp.sum(
        jnp.where(picked, jnp.broadcast_to(r[:, 7:8, :], shape), 0.0), axis=2, keepdims=True
    )
    tops, totals = stats[:, :4], stats[:, 4:]
    highest = jnp.maximum(jnp.max(tops, axis=0), new_score)
    factors = jnp.exp(tops - highest[None])
    weight = jnp.exp(new_score - highest)
    denom = jnp.sum(factors * totals, axis=0) + weight
    summed = jnp.sum(factors * r[:, :4, :], axis=0) + weight.astype(BF16).astype(F32) * value
    result = (summed / denom).astype(BF16).astype(F32)
    for j in range(4):
        attended_ref[:, j * HD : (j + 1) * HD] = result[j : j + 1].astype(BF16)


def local(
    hidden,
    key_value_weight,
    adapter_down_maps,
    adapter_up_maps,
    session_slot,
    lengths,
    queries,
    cached_key_rows,
    cached_value_rows,
):
    n_sess = lax.axis_size("sess")
    n_tensor = lax.axis_size("tensor")
    t = lax.axis_index("tensor")
    slots, two, ranks, width = adapter_down_maps.shape
    shape = jax.ShapeDtypeStruct
    half = width // 2

    parts, own_queries, index, shared, own, hidden = pl.pallas_call(
        spread_kernel,
        out_shape=(
            pltpu.HBM((n_sess, 16, half // 16), BF16),
            shape((8, HD), F32),
            pltpu.SMEM((8,), jnp.int32),
            shape((slots, two, ranks, half + KVH * HD + HD), BF16),
            shape((slots, two, ranks, half + KVH * HD), BF16),
            shape(hidden.shape, BF16),
        ),
        in_specs=[HBM] * 5,
        out_specs=(HBM, VMEM, SMEM, VMEM, VMEM, VMEM),
        scratch_shapes=[
            pltpu.SMEM((n_sess,), jnp.int32),
            pltpu.VMEM(queries.shape, BF16),
            pltpu.VMEM((n_sess, 16, half // 16), BF16),
            pltpu.SemaphoreType.DMA((7,)),
            pltpu.SemaphoreType.DMA((4,)),
        ],
        cost_estimate=pl.CostEstimate(flops=10**5, bytes_accessed=10**5, transcendentals=0),
        compiler_params=pltpu.CompilerParams(vmem_limit_bytes=10 * 1024 * 1024),
    )(
        *(
            pltpu.with_memory_space_constraint(x, pltpu.HBM)
            for x in (
                session_slot,
                hidden,
                queries,
                adapter_down_maps,
                adapter_up_maps,
            )
        )
    )
    parts = lax.all_to_all(parts, "sess", 0, 0, tiled=True)

    other_core = [(i, i ^ 1) for i in range(n_tensor)]
    shared = lax.ppermute(shared, "tensor", other_core)
    pair = own_queries + shared[0, :, :, half + KVH * HD :].reshape(8, HD).astype(F32)
    pair = pair[None]
    def come(x, distance):
        return lax.ppermute(
            x, "tensor", [(i, (i - 2 * distance) % n_tensor) for i in range(n_tensor)]
        )

    near = jnp.concatenate([come(pair, -3), pair, come(pair, 3)])
    before, after = come(near, -1), come(near, 1)

    mine = call(
        reduce_kernel,
        shape((slots * two * 2, ranks, HD), F32),
        [SMEM, VMEM, VMEM, VMEM, ANY],
        [index, parts, own, shared, near],
        10**6,
    )
    other = lax.ppermute(mine, "tensor", other_core)
    terms, mark = call(
        lift_kernel,
        (pltpu.HBM((n_sess, KVH, HD), F32), pltpu.SMEM((8,), jnp.int32)),
        [SMEM, VMEM, VMEM, VMEM, VMEM],
        [index, mine, other, own, shared],
        10**6,
    )
    terms = lax.all_to_all(terms, "sess", 0, 0, tiled=True)

    partial = call(
        attention_kernel,
        shape((n_tensor, 8, HD), F32),
        [SMEM, SMEM, VMEM, VMEM, VMEM, VMEM, VMEM],
        [lengths, mark, before, near, after, cached_key_rows, cached_value_rows],
        10**7,
    )
    base = call(
        base_kernel,
        shape((1, HD), F32),
        [SMEM, VMEM, VMEM],
        [mark, hidden, pltpu.with_memory_space_constraint(key_value_weight, pltpu.HBM)],
        10**4,
    )
    packed = call(
        pack_kernel,
        shape((n_tensor, 8, HD), F32),
        [SMEM, VMEM, VMEM, VMEM],
        [index, terms, base, partial],
        10**5,
    )
    packed = lax.all_to_all(packed, "tensor", 0, 0, tiled=True)

    inverse = jnp.exp(-(2.0 * jnp.arange(HD // 2, dtype=F32) / HD) * math.log(ROPE_BASE))
    angles = lengths[0].astype(F32) * inverse
    cosine, sine = jnp.cos(angles), jnp.sin(angles)
    cosine = jnp.concatenate([cosine, cosine])
    sine = jnp.concatenate([-sine, sine])
    keyed = t < KVH
    rot = jnp.stack(
        [cosine, sine, jnp.where(keyed, cosine, 1.0), jnp.where(keyed, sine, 0.0)]
    )
    return call(
        merge_kernel,
        (shape((1, HD), BF16), shape((1, 4 * HD), BF16)),
        [VMEM, VMEM, VMEM],
        [rot, queries, packed],
        10**5,
    )


def solution(mesh):
    return jax.shard_map(
        local,
        mesh=mesh,
        in_specs=(
            P("sess", None),
            P(None, "tensor"),
            P("sess", None, "tensor", None),
            P("sess", None, "tensor", None),
            P(),
            P("sess"),
            P("sess", "tensor"),
            P("sess", "tensor", None),
            P("sess", "tensor", None),
        ),
        out_specs=(P("sess", "tensor"), P("sess", "tensor")),
        check_vma=False,
    )
```
